512 devices in a mesh: gx: 8 (over z), gy: 8 (over y_lo, x), gz: 8 (over y_hi, core).
Axes of the slice: x: 4, y: 8 (y_hi: 4, y_lo: 2; y = y_hi * 2 + y_lo), z: 8, core: 2. Of those that a mesh axis runs over, the one named last changes fastest.
Arguments:
- populations: float32 [19, 64, 64, 1024], P(None, 'gz', 'gx', 'gy'), may hold values from 0.6 to 1.4
- solid_codes: int32 [64, 64, 1024], P('gz', 'gx', 'gy'), may hold values from 0 to 8
- plane_offsets: int32 [2, 8], replicated, may hold values from 0 to 63
- plane_fractions: int32 [2, 8], replicated, may hold values from 0 to 63
Outputs:
- populations_next: float32 [19, 64, 64, 1024], P(None, 'gz', 'gx', 'gy')
The draws below stay inside these ranges and needn't reach their ends.
All inputs are finite; a program needn't handle non-finite values.
Results may differ from the reference program's by a relative error of at most 0.0001.
Values sent between devices are 32-bit elements; how exact they have to be, the bound alone decides.
No kernel may reach another device: no remote copies, remote signals or barrier semaphores. Data moves between devices by JAX's collectives and lax.ppermute only.
A program may use at most 64 MiB of HBM per device.

```python
import jax
import jax.numpy as jnp

Q = 19
CZ = 8
STEPS = 2
LEVELS = 8
FRAC_DEN = 64
NX = 64
NY = 1024
NZ = 64
PLANES = 8
N_GZ = 8


def plant(drawn, key, smallest, high):
    longest = drawn.shape.index(max(drawn.shape))
    spots = []
    for shift in (0, 1):
        where = [jax.random.randint(jax.random.fold_in(key, axis), (), 0, length) for axis, length in enumerate(drawn.shape)]
        where[longest] = (where[longest] + shift) % drawn.shape[longest]
        spots.append(tuple(where))
    return drawn.at[spots[0]].set(smallest).at[spots[1]].set(high)


def shard_levels(own_key, dims, pieces, low, top_value):
    loudness = 1.0
    for axis_at, blocks in pieces:
        draws = jax.random.uniform(jax.random.fold_in(jax.random.fold_in(own_key, 6), axis_at), (blocks,), jnp.float32, low / len(pieces), top_value / len(pieces))
        loudness = loudness * jnp.repeat(jnp.exp(draws), dims[axis_at] // blocks).reshape((-1,) + (1,) * (len(dims) - 1 - axis_at))
    return loudness


def setup_inputs(seed: int = 0) -> dict:
    keys = jax.random.split(jax.random.key(seed), 5)
    return {
        "populations": jnp.clip(0.6 + 0.79999995 * jax.random.uniform(keys[0], (Q, NZ, NX, NY), jnp.float32) ** shard_levels(keys[0], (Q, NZ, NX, NY), ((1, 8), (2, 8), (3, 8)), -0.2, 0.2), 0.6, 1.4),
        "solid_codes": plant(jax.random.randint(keys[1], (NZ, NX, NY), 0, LEVELS + 1), jax.random.fold_in(keys[1], 1), 0, LEVELS).astype(jnp.int32),
        "plane_offsets": plant(jax.random.randint(keys[2], (STEPS, PLANES), 0, NX), jax.random.fold_in(keys[2], 1), 0, NX - 1).astype(jnp.int32),
        "plane_fractions": plant(jax.random.randint(keys[3], (STEPS, PLANES), 0, FRAC_DEN), jax.random.fold_in(keys[3], 1), 0, FRAC_DEN - 1).astype(jnp.int32),
    }


velocities = ((0, 0, 0), (1, 0, 0), (-1, 0, 0), (0, 1, 0), (0, -1, 0), (0, 0, 1), (0, 0, -1), (1, 1, 0), (-1, -1, 0), (1, -1, 0), (-1, 1, 0), (1, 0, 1), (-1, 0, -1), (1, 0, -1), (-1, 0, 1), (0, 1, 1), (0, -1, -1), (0, 1, -1), (0, -1, 1))
lattice_weights = (1.0 / 3.0,) + (1.0 / 18.0,) * 6 + (1.0 / 36.0,) * 12
opposite_index = (0, 2, 1, 4, 3, 6, 5, 8, 7, 10, 9, 12, 11, 14, 13, 16, 15, 18, 17)
relax_time = 0.9
rising = (5, 11, 14, 15, 18)
sinking = (6, 12, 13, 16, 17)


def velocity_sum(distribution, component):
    total = jnp.zeros_like(distribution[0])
    for popul_index in range(19):
        moving = velocities[popul_index][component]
        if moving == 1:
            total = total + distribution[popul_index]
        elif moving == -1:
            total = total - distribution[popul_index]
    return total


def collide(distribution, solid_codes):
    solid = solid_codes.astype(jnp.float32) / LEVELS
    density = jnp.sum(distribution, axis=0)
    speed_x = velocity_sum(distribution, 0) / density
    speed_y = velocity_sum(distribution, 1) / density
    speed_z = velocity_sum(distribution, 2) / density
    square = speed_x * speed_x + speed_y * speed_y + speed_z * speed_z
    outgoing = []
    for popul_index in range(19):
        move_x, move_y, move_z = velocities[popul_index]
        along = move_x * speed_x + move_y * speed_y + move_z * speed_z
        balance = lattice_weights[popul_index] * density * (1.0 + 3.0 * along + 4.5 * along * along - 1.5 * square)
        relaxed = distribution[popul_index] - (distribution[popul_index] - balance) / relax_time
        outgoing.append((1.0 - solid) * relaxed + solid * distribution[opposite_index[popul_index]])
    return jnp.stack(outgoing)


def forward_move(layer_in, offset_in, weight_in):
    return (1.0 - weight_in) * jnp.roll(layer_in, offset_in, axis=1) + weight_in * jnp.roll(layer_in, offset_in + 1, axis=1)


def backward_move(layer_in, offset_in, weight_in):
    return (1.0 - weight_in) * jnp.roll(layer_in, -offset_in, axis=1) + weight_in * jnp.roll(layer_in, -offset_in - 1, axis=1)


def advance(distribution, solid_codes, offsets, fractions):
    collided = collide(distribution, solid_codes)
    blocks = collided.reshape(19, N_GZ, CZ, NX, NY)
    fraction = fractions.astype(jnp.float32) / FRAC_DEN
    top_layers = jnp.stack([blocks[popul_index, :, CZ - 1] for popul_index in rising])
    bottoms = jnp.stack([blocks[popul_index, :, 0] for popul_index in sinking])
    next_offset = jnp.roll(offsets, -1)
    next_fraction = jnp.roll(fraction, -1)
    raised = jax.vmap(forward_move, in_axes=(1, 0, 0), out_axes=1)(top_layers, next_offset, next_fraction)
    lowered = jax.vmap(backward_move, in_axes=(1, 0, 0), out_axes=1)(bottoms, offsets, fraction)
    from_below = jnp.roll(raised, 1, axis=1)
    from_above = jnp.roll(lowered, -1, axis=1)
    arrived = []
    for popul_index in range(19):
        move_x, move_y, move_z = velocities[popul_index]
        middle = blocks[popul_index]
        if move_z == 1:
            source = jnp.concatenate([from_below[rising.index(popul_index)][:, None], middle[:, :CZ - 1]], axis=1)
        elif move_z == -1:
            source = jnp.concatenate([middle[:, 1:], from_above[sinking.index(popul_index)][:, None]], axis=1)
        else:
            source = middle
        arrived.append(jnp.roll(source, (move_x, move_y), axis=(2, 3)))
    return jnp.stack(arrived).reshape(19, NZ, NX, NY)


def reference(populations, solid_codes, plane_offsets, plane_fractions):
    weights = jnp.asarray(lattice_weights, jnp.float32)[:, None, None, None]
    distribution = populations * weights
    for step_index in range(STEPS):
        distribution = advance(distribution, solid_codes, plane_offsets[step_index], plane_fractions[step_index])
    return distribution / weights
```

```python
import jax
import jax.numpy as jnp
from jax import lax
from jax.experimental import pallas as pl
from jax.experimental.pallas import tpu as pltpu
from jax.sharding import PartitionSpec as P

LEVELS = 8
FRAC_DEN = 64
velocities = (
    (0, 0, 0), (1, 0, 0), (-1, 0, 0), (0, 1, 0), (0, -1, 0), (0, 0, 1), (0, 0, -1),
    (1, 1, 0), (-1, -1, 0), (1, -1, 0), (-1, 1, 0), (1, 0, 1), (-1, 0, -1), (1, 0, -1),
    (-1, 0, 1), (0, 1, 1), (0, -1, -1), (0, 1, -1), (0, -1, 1),
)
weight_inverse = (3.0,) + (18.0,) * 6 + (36.0,) * 12
lattice_weights = tuple(1.0 / v for v in weight_inverse)
relax_time = 0.9
pairs = ((1, 2), (3, 4), (5, 6), (7, 8), (9, 10), (11, 12), (13, 14), (15, 16), (17, 18))
rising = (5, 11, 14, 15, 18)
sinking = (6, 13, 12, 17, 16)
level = (0, 1, 2, 3, 4, 7, 8, 9, 10)
forward = (1, 7, 9, 11, 13)
backward = (2, 8, 10, 12, 14)
F32 = jnp.float32


def roll(value, by, axis):
    if isinstance(by, int):
        by %= value.shape[axis]
        if by == 0:
            return value
    return pltpu.roll(value, by, axis)


def lanes(shape=(8, 128)):
    return lax.broadcasted_iota(jnp.int32, shape, 1)


def rows(shape=(8, 128)):
    return lax.broadcasted_iota(jnp.int32, shape, 0)


def collide(f, solid):
    density = f[0]
    for i, j in pairs:
        density = density + (f[i] + f[j])
    inverse = 1.0 / density
    speed = []
    for axis in range(3):
        total = None
        for i, j in pairs:
            moving = velocities[i][axis]
            if moving == 0:
                continue
            part = f[i] - f[j] if moving == 1 else f[j] - f[i]
            total = part if total is None else total + part
        speed.append(total * inverse)
    square = speed[0] * speed[0] + speed[1] * speed[1] + speed[2] * speed[2]
    fluid = 1.0 - solid
    keep = fluid * (1.0 - 1.0 / relax_time)
    pull = fluid * density * (1.0 / relax_time)
    calm = pull - 1.5 * square * pull
    post = [None] * 19
    post[0] = keep * f[0] + lattice_weights[0] * calm + solid * f[0]
    for i, j in pairs:
        along = None
        for axis in range(3):
            moving = velocities[i][axis]
            if moving == 0:
                continue
            if along is None:
                along = speed[axis] if moving == 1 else -speed[axis]
            else:
                along = along + speed[axis] if moving == 1 else along - speed[axis]
        weight = lattice_weights[i]
        flow = (3.0 * weight) * (pull * along)
        even = weight * calm + (1.5 * flow) * along
        post[i] = keep * f[i] + solid * f[j] + (even + flow)
        post[j] = keep * f[j] + solid * f[i] + (even - flow)
    return post


def edge_kernel(pops, codes, out):
    lane = lanes()
    for tile in range(5):
        packed = jnp.zeros((8, 128), F32)
        for slot in range(4):
            item = tile * 4 + slot
            for z in range(8):
                start = slot * 32 + z * 4
                source = pops[item, z] if item < 19 else codes[z].astype(F32)
                moved = roll(source, start + 2, 1)
                packed = jnp.where(lane < start, packed, moved)
        out[tile] = packed


def first_kernel(pops, codes, left, right, p1, side, chunks, ahead, behind):
    lane = lanes()
    outer = []
    for tile in range(5):
        both = jnp.where(lane % 4 < 2, left[tile], right[tile])
        for slot in range(4):
            outer.append(roll(both, -32 * slot, 1))
    beside = collide([outer[i] * lattice_weights[i] for i in range(19)], outer[19] * (1.0 / LEVELS))
    shifted = []
    for i in range(19):
        shifted.append(roll(beside[i], velocities[i][1], 1))
    for z in range(8):
        f = [pops[i, z] * lattice_weights[i] for i in range(19)]
        post = collide(f, codes[z].astype(F32) * (1.0 / LEVELS))
        for i in range(19):
            step = velocities[i][1]
            value = post[i]
            if step == 1:
                shifted[i] = jnp.where(lane == 4 * z + 2, roll(value, 4 * z + 3, 1), shifted[i])
                value = jnp.where(lane == 0, roll(beside[i], -(4 * z + 1), 1), roll(value, 1, 1))
            elif step == -1:
                shifted[i] = jnp.where(lane == 4 * z + 1, roll(value, 4 * z + 1, 1), shifted[i])
                value = jnp.where(lane == 127, roll(beside[i], 127 - (4 * z + 2), 1), roll(value, -1, 1))
            p1[i, z] = value
            if i in forward:
                ahead[forward.index(i), z : z + 1, :] = value[7:8, :]
            if i in backward:
                behind[backward.index(i), z : z + 1, :] = value[0:1, :]
    for i in range(19):
        side[i] = shifted[i]
    side[19] = outer[19]
    for slot in range(5):
        ahead[5, slot : slot + 1, :] = shifted[forward[slot]][7:8, :]
        behind[5, slot : slot + 1, :] = shifted[backward[slot]][0:1, :]
    for slot in range(5, 8):
        ahead[5, slot : slot + 1, :] = jnp.zeros((1, 128), F32)
        behind[5, slot : slot + 1, :] = jnp.zeros((1, 128), F32)
    upper = [(i, 7) for i in rising] + [(i, 7) for i in level] + [(i, 6) for i in rising] + [(19, 7)]
    lower = [(i, 0) for i in sinking] + [(i, 0) for i in level] + [(i, 1) for i in sinking] + [(19, 0)]
    for group, items in enumerate((upper, lower)):
        for tile in range(3):
            held = [jnp.zeros((8, 128), F32)] * 8
            for slot, (i, z) in enumerate(items[tile * 7 : tile * 7 + 7]):
                main = p1[i, z] if i < 19 else codes[z].astype(F32)
                extra = shifted[i] if i < 19 else outer[19]
                first = jnp.where(lane == 127, roll(extra, 127 - (4 * z + 1), 1), main)
                last = jnp.where(lane == 0, roll(extra, -(4 * z + 2), 1), main)
                for d in range(8):
                    source = first if d == 0 else last if d == 7 else main
                    moved = roll(source, 18 * slot - 16 * d + 1, 1)
                    held[d] = jnp.where(lane < 18 * slot, held[d], moved)
            for d in range(8):
                chunks[d, group * 3 + tile] = held[d]


def cross(outgoing, lane, shift_a, shift_b, frac_a, frac_b):
    length = outgoing.shape[0]
    low = (lane // 32) % 2 == 1
    up_a, down_a = roll(outgoing, shift_a, 0), roll(outgoing, (length - shift_a) % length, 0)
    up_b, down_b = roll(outgoing, shift_b, 0), roll(outgoing, (length - shift_b) % length, 0)
    near = jnp.where(lane < 64, jnp.where(low, down_a, up_a), jnp.where(low, down_b, up_b))
    far = jnp.where(low, roll(near, -1, 0), roll(near, 1, 0))
    share = jnp.where(lane < 64, frac_a, frac_b)
    mixed = (1.0 - share) * near + share * far
    return jnp.where(low, roll(mixed, 32, 1), roll(mixed, -32, 1))


def plane_kernel(offsets, fractions, own, below, above, out, work, state):
    length = work.shape[1]
    lane8 = lanes()
    lane = lanes((length, 128))
    here = lax.axis_index("gz")
    after = (here + 1) % lax.axis_size("gz")

    def params(step):
        return (
            offsets[step, here],
            offsets[step, after],
            fractions[step, here].astype(F32) * (1.0 / FRAC_DEN),
            fractions[step, after].astype(F32) * (1.0 / FRAC_DEN),
        )

    for item in range(20):
        tile, slot = divmod(item, 7)
        for b in range(8):
            sets = (below[b, tile], own[b, 3 + tile], own[b, tile], above[b, tile])
            moved = [roll(s, 32 * q - 18 * slot, 1) for q, s in enumerate(sets)]
            value = jnp.where(
                lane8 < 64,
                jnp.where(lane8 < 32, moved[0], moved[1]),
                jnp.where(lane8 < 96, moved[2], moved[3]),
            )
            work[item, 8 * b : 8 * b + 8, :] = value
    for j in range(5):
        step_x = velocities[rising[j]][0]
        state[sinking[j]] = roll(cross(work[j], lane, *params(0)), step_x, 0)
        state[rising[j]] = roll(work[14 + j], step_x, 0)
    for k, i in enumerate(level):
        state[i] = roll(work[5 + k], velocities[i][0], 0)
    for b in range(8):
        at = slice(8 * b, 8 * b + 8)
        post = collide([state[i, at, :] for i in range(19)], work[19, at, :] * (1.0 / LEVELS))
        for i in range(19):
            state[i, at, :] = roll(post[i], velocities[i][1], 1)
    final = []
    for i in level:
        final.append((i, None))
    for j in range(5):
        final.append((sinking[j], None))
    for j in range(5):
        final.append((rising[j], j))
    for n, (i, crossing) in enumerate(final):
        value = state[i]
        if crossing is not None:
            value = cross(value, lane, *params(1))
        work[n] = roll(value, velocities[i][0], 0)
    for b in range(8):
        for tile in range(5):
            packed = jnp.zeros((8, 128), F32)
            for slot in range(8):
                n = tile * 8 + slot
                if n >= 38:
                    break
                group, q = (n, 2) if n < 19 else (n - 19, 1)
                moved = roll(work[group, 8 * b : 8 * b + 8, :], 16 * slot - 32 * q - 1, 1)
                packed = jnp.where(lane8 < 16 * slot, packed, moved)
            out[b, tile] = packed


def streamed_x(source, z, i, from_behind, from_ahead, row):
    value = source[i, z]
    if i in forward:
        j = forward.index(i)
        return jnp.where(row == 0, jnp.broadcast_to(from_behind[j, z + 0 : z + 1, :], (8, 128)), roll(value, 1, 0))
    if i in backward:
        j = backward.index(i)
        return jnp.where(row == 7, jnp.broadcast_to(from_ahead[j, z + 0 : z + 1, :], (8, 128)), roll(value, -1, 0))
    return value


def inner_kernel(p1, side, codes, from_behind, from_ahead, p2, ahead, behind):
    lane, row = lanes(), rows()
    f = []
    for i in range(19):
        value = side[i]
        if i in forward:
            j = forward.index(i)
            value = jnp.where(row == 0, jnp.broadcast_to(from_behind[5, j : j + 1, :], (8, 128)), roll(value, 1, 0))
        elif i in backward:
            j = backward.index(i)
            value = jnp.where(row == 7, jnp.broadcast_to(from_ahead[5, j : j + 1, :], (8, 128)), roll(value, -1, 0))
        f.append(roll(value, 4 * velocities[i][2], 1))
    beside = collide(f, side[19] * (1.0 / LEVELS))
    for j in range(5):
        for z in (0, 7):
            ahead[j, z : z + 1, :] = jnp.zeros((1, 128), F32)
            behind[j, z : z + 1, :] = jnp.zeros((1, 128), F32)
    for z in range(1, 7):
        f = [streamed_x(p1, z - velocities[i][2], i, from_behind, from_ahead, row) for i in range(19)]
        post = collide(f, codes[z].astype(F32) * (1.0 / LEVELS))
        for i in range(19):
            step = velocities[i][1]
            value = post[i]
            if step == 1:
                value = jnp.where(lane == 0, roll(beside[i], -(4 * z + 1), 1), roll(value, 1, 1))
            elif step == -1:
                value = jnp.where(lane == 127, roll(beside[i], 127 - (4 * z + 2), 1), roll(value, -1, 1))
            p2[i, z] = value
            if i in forward:
                ahead[forward.index(i), z : z + 1, :] = value[7:8, :]
            if i in backward:
                behind[backward.index(i), z : z + 1, :] = value[0:1, :]
    for i in range(19):
        for z in (0, 7):
            p2[i, z] = jnp.zeros((8, 128), F32)


def last_kernel(p2, from_behind, from_ahead, planes, out):
    lane, row = lanes(), rows()
    for i in range(19):
        for z in range(8):
            source = z - velocities[i][2]
            if 1 <= source <= 6:
                out[i, z] = streamed_x(p2, source, i, from_behind, from_ahead, row) * weight_inverse[i]
    target = []
    for group in range(2):
        z, inner = (7, 6) if group == 0 else (0, 1)
        inward, outward = (sinking, rising) if group == 0 else (rising, sinking)
        target += [(i, z) for i in level] + [(i, inner) for i in inward] + [(i, z) for i in inward]
    part = lane // 16
    for tile in range(5):
        held = [planes[h, tile] for h in range(8)]
        for k in (1, 2, 4):
            fixed = part & k == 0
            for h in range(8):
                if h & k == 0:
                    lo, hi = held[h], held[h | k]
                    held[h] = jnp.where(fixed, lo, roll(hi, 16 * k, 1))
                    held[h | k] = jnp.where(fixed, roll(lo, -16 * k, 1), hi)
        for slot in range(8):
            n = tile * 8 + slot
            if n < 38:
                i, z = target[n]
                out[i, z] = held[slot] * weight_inverse[i]


def run(kernel, outs, args, scalars=0, scratch=()):
    specs = [pl.BlockSpec(memory_space=pltpu.SMEM)] * scalars
    specs += [pl.BlockSpec(memory_space=pltpu.VMEM)] * (len(args) - scalars)
    shapes = [jax.ShapeDtypeStruct(s, F32) for s in outs]
    return pl.pallas_call(
        kernel,
        out_shape=shapes,
        in_specs=specs,
        out_specs=[pl.BlockSpec(memory_space=pltpu.VMEM)] * len(outs),
        scratch_shapes=[pltpu.VMEM(s, F32) for s in scratch],
        compiler_params=pltpu.CompilerParams(vmem_limit_bytes=32 * 1024 * 1024),
    )(*args)


def neighbours(value_up, value_down, axis):
    peers = lax.axis_size(axis)
    up = [(i, (i + 1) % peers) for i in range(peers)]
    down = [(j, i) for i, j in up]
    return lax.ppermute(value_up, axis, up), lax.ppermute(value_down, axis, down)


def body(pops, codes, offsets, fractions):
    tile = (8, 128)
    (edges,) = run(edge_kernel, [(5,) + tile], (pops, codes))
    left, right = neighbours(edges, edges, "gy")
    p1, side, chunks, ahead, behind = run(
        first_kernel,
        [(19, 8) + tile, (20,) + tile, (8, 6) + tile, (6,) + tile, (6,) + tile],
        (pops, codes, left, right),
    )
    own = lax.all_to_all(chunks, "gx", 0, 0)
    from_behind, from_ahead = neighbours(ahead, behind, "gx")
    below, above = neighbours(own[:, 0:3], own[:, 3:6], "gz")
    p2, ahead, behind = run(
        inner_kernel,
        [(19, 8) + tile, (5,) + tile, (5,) + tile],
        (p1, side, codes, from_behind, from_ahead),
    )
    (planes,) = run(
        plane_kernel,
        [(8, 5) + tile],
        (offsets, fractions, own, below, above),
        scalars=2,
        scratch=[(20, 64, 128), (19, 64, 128)],
    )
    planes = lax.all_to_all(planes, "gx", 0, 0)
    from_behind, from_ahead = neighbours(ahead, behind, "gx")
    (out,) = run(last_kernel, [(19, 8) + tile], (p2, from_behind, from_ahead, planes))
    return out


def solution(mesh):
    in_specs = (P(None, "gz", "gx", "gy"), P("gz", "gx", "gy"), P(), P())
    out_specs = P(None, "gz", "gx", "gy")
    return jax.shard_map(body, mesh=mesh, in_specs=in_specs, out_specs=out_specs, check_vma=False)
```

```python
import jax
import jax.numpy as jnp
from jax import lax
from jax.experimental import pallas as pl
from jax.experimental.pallas import tpu as pltpu
from jax.sharding import PartitionSpec as P

LEVELS = 8
FRAC_DEN = 64
velocities = (
    (0, 0, 0), (1, 0, 0), (-1, 0, 0), (0, 1, 0), (0, -1, 0), (0, 0, 1), (0, 0, -1),
    (1, 1, 0), (-1, -1, 0), (1, -1, 0), (-1, 1, 0), (1, 0, 1), (-1, 0, -1), (1, 0, -1),
    (-1, 0, 1), (0, 1, 1), (0, -1, -1), (0, 1, -1), (0, -1, 1),
)
weight_inverse = (3.0,) + (18.0,) * 6 + (36.0,) * 12
lattice_weights = tuple(1.0 / v for v in weight_inverse)
relax_time = 0.9
pairs = ((1, 2), (3, 4), (5, 6), (7, 8), (9, 10), (11, 12), (13, 14), (15, 16), (17, 18))
rising = (5, 11, 14, 15, 18)
sinking = (6, 13, 12, 17, 16)
level = (0, 1, 2, 3, 4, 7, 8, 9, 10)
forward = (1, 7, 9, 11, 13)
backward = (2, 8, 10, 12, 14)
sideways = (3, 4, 7, 8, 9, 10, 15, 16, 17, 18)
F32 = jnp.float32


def roll(value, by, axis):
    if isinstance(by, int):
        by %= value.shape[axis]
        if by == 0:
            return value
    return pltpu.roll(value, by, axis)


def lanes(shape=(8, 128)):
    return lax.broadcasted_iota(jnp.int32, shape, 1)


def rows(shape=(8, 128)):
    return lax.broadcasted_iota(jnp.int32, shape, 0)


def collide(f, solid):
    density = f[0]
    for i, j in pairs:
        density = density + (f[i] + f[j])
    inverse = 1.0 / density
    speed = []
    for axis in range(3):
        total = None
        for i, j in pairs:
            moving = velocities[i][axis]
            if moving == 0:
                continue
            part = f[i] - f[j] if moving == 1 else f[j] - f[i]
            total = part if total is None else total + part
        speed.append(total * inverse)
    square = speed[0] * speed[0] + speed[1] * speed[1] + speed[2] * speed[2]
    fluid = 1.0 - solid
    keep = fluid * (1.0 - 1.0 / relax_time)
    pull = fluid * density * (1.0 / relax_time)
    calm = pull - 1.5 * square * pull
    post = [None] * 19
    post[0] = keep * f[0] + lattice_weights[0] * calm + solid * f[0]
    for i, j in pairs:
        along = None
        for axis in range(3):
            moving = velocities[i][axis]
            if moving == 0:
                continue
            if along is None:
                along = speed[axis] if moving == 1 else -speed[axis]
            else:
                along = along + speed[axis] if moving == 1 else along - speed[axis]
        weight = lattice_weights[i]
        flow = (3.0 * weight) * (pull * along)
        even = weight * calm + (1.5 * flow) * along
        post[i] = keep * f[i] + solid * f[j] + (even + flow)
        post[j] = keep * f[j] + solid * f[i] + (even - flow)
    return post


def edge_kernel(pops, codes, out):
    lane = lanes()
    for tile in range(5):
        packed = jnp.zeros((8, 128), F32)
        for slot in range(4):
            item = tile * 4 + slot
            for z in range(8):
                start = slot * 32 + z * 4
                source = pops[item, z] if item < 19 else codes[z].astype(F32)
                moved = roll(source, start + 2, 1)
                packed = jnp.where(lane < start, packed, moved)
        out[tile] = packed


UPPER = [(i, 7) for i in rising] + [(i, 7) for i in level] + [(i, 6) for i in rising] + [(19, 7)]
LOWER = [(i, 0) for i in sinking] + [(i, 0) for i in level] + [(i, 1) for i in sinking] + [(19, 0)]
NEAR = [(group, tile, slot, i, z) for group, items in enumerate((UPPER, LOWER)) for tile in range(3) for slot, (i, z) in enumerate(items[7 * tile : 7 * tile + 7])]
AHEAD_ROW, BEHIND_ROW = slice(7, 8), slice(0, 1)


def row_place(j, z):
    r = 6 * j + z - 1
    return r // 8, slice(r % 8, r % 8 + 1)


def main_kernel(pops, codes, p1, wrapped, chunks, ahead, behind):
    lane = lanes()
    side = [jnp.zeros((8, 128), F32) for _ in range(19)]
    for z in range(8):
        f = [pops[i, z] * lattice_weights[i] for i in range(19)]
        post = collide(f, codes[z].astype(F32) * (1.0 / LEVELS))
        for i in range(19):
            step = velocities[i][1]
            value = roll(post[i], step, 1)
            if step == 1:
                side[i] = jnp.where(lane == 4 * z + 2, roll(value, 4 * z + 2, 1), side[i])
            elif step == -1:
                side[i] = jnp.where(lane == 4 * z + 1, roll(value, 4 * z + 2, 1), side[i])
            p1[i, z] = value
            target = z + velocities[i][2]
            if 1 <= target <= 6 and i in forward:
                tile, at = row_place(forward.index(i), target)
                ahead[tile, at, :] = value[AHEAD_ROW, :]
            if 1 <= target <= 6 and i in backward:
                tile, at = row_place(backward.index(i), target)
                behind[tile, at, :] = value[BEHIND_ROW, :]
    for k, i in enumerate(sideways):
        wrapped[k] = side[i]
    for group in range(2):
        for tile in range(3):
            held = [jnp.zeros((8, 128), F32)] * 6
            for _, _, slot, i, z in [n for n in NEAR if n[:2] == (group, tile)]:
                source = p1[i, z] if i < 19 else codes[z].astype(F32)
                for d in range(1, 7):
                    moved = roll(source, 18 * slot - 16 * d + 1, 1)
                    held[d - 1] = jnp.where(lane < 18 * slot, held[d - 1], moved)
            for d in range(6):
                chunks[d, group * 3 + tile] = held[d]


def edge_kernel_2(left, right, p1, codes, wrapped, middle, ahead, behind, chunks, post_side, side):
    lane = lanes()
    ends = (lane == 0) | (lane == 127)
    me, peers = lax.axis_index("gx"), lax.axis_size("gx")
    after, before = (me + 1) % peers, (me + peers - 1) % peers
    for tile in range(4):
        chunks[after, 6 + tile] = ahead[tile]
        chunks[before, 6 + tile] = behind[tile]
    for d in range(1, 7):
        for tile in range(6):
            chunks[d, tile] = middle[d - 1, tile]
    outer = []
    for tile in range(5):
        both = jnp.where(lane % 4 < 2, left[tile], right[tile])
        for slot in range(4):
            outer.append(roll(both, -32 * slot, 1))
    beside = collide([outer[i] * lattice_weights[i] for i in range(19)], outer[19] * (1.0 / LEVELS))
    beside.append(outer[19])
    shifted = list(beside)
    for k, i in enumerate(sideways):
        step = velocities[i][1]
        shifted[i] = jnp.where(lane % 4 == (2 if step == 1 else 1), wrapped[k], roll(beside[i], step, 1))
    for i in range(20):
        side[i] = shifted[i]
        post_side[i] = beside[i]
    row_lane = lanes((1, 128))
    for members, to, source, at_x in ((forward, after, ahead, AHEAD_ROW), (backward, before, behind, BEHIND_ROW)):
        extra = [jnp.zeros((1, 128), F32)] * 2
        for j, i in enumerate(members):
            extra[j // 4] = jnp.where(row_lane // 32 == j % 4, roll(shifted[i][at_x, :], 32 * (j % 4), 1), extra[j // 4])
            step = velocities[i][1]
            if step == 0:
                continue
            for z in range(1, 7):
                tile, at = row_place(j, z)
                lane_at, start = (0, 4 * z + 1) if step == 1 else (127, 4 * z + 2)
                fixed = roll(beside[i][at_x, :], lane_at - start, 1)
                chunks[to, 6 + tile, at, :] = jnp.where(row_lane == lane_at, fixed, source[tile, at, :])
        chunks[to, 9, 6:7, :] = extra[0]
        chunks[to, 9, 7:8, :] = extra[1]
    for group in range(2):
        for tile in range(3):
            held = [jnp.zeros((8, 128), F32)] * 2
            for _, _, slot, i, z in [n for n in NEAR if n[:2] == (group, tile)]:
                main = p1[i, z] if i < 19 else codes[z].astype(F32)
                step = velocities[i][1] if i < 19 else 0
                first = last = main
                if step == 1:
                    first = jnp.where(ends, roll(beside[i], 127 - 4 * z, 1), main)
                elif step == -1:
                    last = jnp.where(ends, roll(beside[i], 125 - 4 * z, 1), main)
                else:
                    first = jnp.where(lane == 127, roll(beside[i], 126 - 4 * z, 1), main)
                    last = jnp.where(lane == 0, roll(beside[i], -(4 * z + 2), 1), main)
                held[0] = jnp.where(lane < 18 * slot, held[0], roll(first, 18 * slot + 1, 1))
                held[1] = jnp.where(lane < 18 * slot, held[1], roll(last, 18 * slot - 111, 1))
            chunks[0, group * 3 + tile] = held[0]
            chunks[7, group * 3 + tile] = held[1]


def cross(outgoing, lane, shift_a, shift_b, frac_a, frac_b):
    length = outgoing.shape[0]
    low = (lane // 32) % 2 == 1
    up_a, down_a = roll(outgoing, shift_a, 0), roll(outgoing, (length - shift_a) % length, 0)
    up_b, down_b = roll(outgoing, shift_b, 0), roll(outgoing, (length - shift_b) % length, 0)
    near = jnp.where(lane < 64, jnp.where(low, down_a, up_a), jnp.where(low, down_b, up_b))
    far = jnp.where(low, roll(near, -1, 0), roll(near, 1, 0))
    share = jnp.where(lane < 64, frac_a, frac_b)
    mixed = (1.0 - share) * near + share * far
    return jnp.where(low, roll(mixed, 32, 1), roll(mixed, -32, 1))


def spread_kernel(own, work):
    lane8 = lanes()
    for item in range(20):
        tile, slot = divmod(item, 7)
        for b in range(8):
            value = jnp.where(
                lane8 < 64,
                roll(own[b, 3 + tile], 32 - 18 * slot, 1),
                roll(own[b, tile], 64 - 18 * slot, 1),
            )
            work[item, 8 * b : 8 * b + 8, :] = value


def plane_kernel(offsets, fractions, spread, below, above, ahead, behind, out, work, state):
    length = work.shape[1]
    lane8 = lanes()
    lane = lanes((length, 128))
    here = lax.axis_index("gz")
    after = (here + 1) % lax.axis_size("gz")
    me, peers = lax.axis_index("gx"), lax.axis_size("gx")
    for tile in range(4):
        out[(me + 1) % peers, 5 + tile] = ahead[tile]
        out[(me + peers - 1) % peers, 5 + tile] = behind[tile]

    def params(step):
        return (
            offsets[step, here],
            offsets[step, after],
            fractions[step, here].astype(F32) * (1.0 / FRAC_DEN),
            fractions[step, after].astype(F32) * (1.0 / FRAC_DEN),
        )

    for item in range(20):
        tile, slot = divmod(item, 7)
        for b in range(8):
            at = slice(8 * b, 8 * b + 8)
            moved = jnp.where(
                lane8 < 64,
                roll(below[b, tile], -18 * slot, 1),
                roll(above[b, tile], 96 - 18 * slot, 1),
            )
            work[item, at, :] = jnp.where((lane8 >= 32) & (lane8 < 96), spread[item, at, :], moved)
    for j in range(5):
        step_x = velocities[rising[j]][0]
        state[sinking[j]] = roll(cross(work[j], lane, *params(0)), step_x, 0)
        state[rising[j]] = roll(work[14 + j], step_x, 0)
    for k, i in enumerate(level):
        state[i] = roll(work[5 + k], velocities[i][0], 0)
    for b in range(8):
        at = slice(8 * b, 8 * b + 8)
        post = collide([state[i, at, :] for i in range(19)], work[19, at, :] * (1.0 / LEVELS))
        for i in range(19):
            state[i, at, :] = roll(post[i], velocities[i][1], 1)
    final = []
    for i in level:
        final.append((i, None))
    for j in range(5):
        final.append((sinking[j], None))
    for j in range(5):
        final.append((rising[j], j))
    for n, (i, crossing) in enumerate(final):
        value = state[i]
        if crossing is not None:
            value = cross(value, lane, *params(1))
        work[n] = roll(value, velocities[i][0], 0)
    for b in range(8):
        for tile in range(5):
            packed = jnp.zeros((8, 128), F32)
            for slot in range(8):
                n = tile * 8 + slot
                if n >= 38:
                    break
                group, q = (n, 2) if n < 19 else (n - 19, 1)
                moved = roll(work[group, 8 * b : 8 * b + 8, :], 16 * slot - 32 * q - 1, 1)
                packed = jnp.where(lane8 < 16 * slot, packed, moved)
            out[b, tile] = packed


def moved_x(value, i, z, rows_behind, rows_ahead, first_tile, row):
    if i in forward:
        tile, at = row_place(forward.index(i), z)
        source, to = rows_behind(first_tile + tile, at), 0
    elif i in backward:
        tile, at = row_place(backward.index(i), z)
        source, to = rows_ahead(first_tile + tile, at), 7
    else:
        return value
    return jnp.where(row == to, jnp.broadcast_to(source, (8, 128)), roll(value, velocities[i][0], 0))


def inner_kernel(p1, post_side, side, codes, own, p2, ahead, behind):
    lane, row = lanes(), rows()
    me, peers = lax.axis_index("gx"), lax.axis_size("gx")
    after, before = (me + 1) % peers, (me + peers - 1) % peers

    def rows_behind(tile, at):
        return own[before, tile, at, :]

    def rows_ahead(tile, at):
        return own[after, tile, at, :]

    f = []
    for i in range(19):
        value = side[i]
        for members, get, to in ((forward, rows_behind, 0), (backward, rows_ahead, 7)):
            if i in members:
                j = members.index(i)
                source = roll(get(9, slice(6 + j // 4, 7 + j // 4)), -32 * (j % 4), 1)
                value = jnp.where(row == to, jnp.broadcast_to(source, (8, 128)), roll(value, velocities[i][0], 0))
        f.append(roll(value, 4 * velocities[i][2], 1))
    beside = collide(f, side[19] * (1.0 / LEVELS))
    for j in range(2):
        ahead[3, 6 + j : 7 + j, :] = jnp.zeros((1, 128), F32)
        behind[3, 6 + j : 7 + j, :] = jnp.zeros((1, 128), F32)

    def mended(value, edge, step, z):
        if step == 1:
            return jnp.where(lane == 0, roll(edge, -(4 * z + 1), 1), value)
        if step == -1:
            return jnp.where(lane == 127, roll(edge, 127 - (4 * z + 2), 1), value)
        return value

    for z in range(1, 7):
        f = []
        for i in range(19):
            source = z - velocities[i][2]
            value = mended(p1[i, source], post_side[i], velocities[i][1], source)
            f.append(moved_x(value, i, z, rows_behind, rows_ahead, 6, row))
        post = collide(f, codes[z].astype(F32) * (1.0 / LEVELS))
        for i in range(19):
            step = velocities[i][1]
            value = mended(roll(post[i], step, 1), beside[i], step, z)
            p2[i, z - 1] = value
            if i in forward:
                tile, at = row_place(forward.index(i), z)
                ahead[tile, at, :] = value[AHEAD_ROW, :]
            if i in backward:
                tile, at = row_place(backward.index(i), z)
                behind[tile, at, :] = value[BEHIND_ROW, :]


def last_kernel(p2, planes, out):
    lane, row = lanes(), rows()
    me, peers = lax.axis_index("gx"), lax.axis_size("gx")
    after, before = (me + 1) % peers, (me + peers - 1) % peers

    def rows_behind(tile, at):
        return planes[before, tile, at, :]

    def rows_ahead(tile, at):
        return planes[after, tile, at, :]

    for i in range(19):
        for z in range(8):
            source = z - velocities[i][2]
            if 1 <= source <= 6:
                value = moved_x(p2[i, source - 1], i, source, rows_behind, rows_ahead, 5, row)
                out[i, z] = value * weight_inverse[i]
    target = []
    for group in range(2):
        z, inner = (7, 6) if group == 0 else (0, 1)
        inward, outward = (sinking, rising) if group == 0 else (rising, sinking)
        target += [(i, z) for i in level] + [(i, inner) for i in inward] + [(i, z) for i in inward]
    part = lane // 16
    for tile in range(5):
        held = [planes[h, tile] for h in range(8)]
        for k in (1, 2, 4):
            fixed = part & k == 0
            for h in range(8):
                if h & k == 0:
                    lo, hi = held[h], held[h | k]
                    held[h] = jnp.where(fixed, lo, roll(hi, 16 * k, 1))
                    held[h | k] = jnp.where(fixed, roll(lo, -16 * k, 1), hi)
        for slot in range(8):
            n = tile * 8 + slot
            if n < 38:
                i, z = target[n]
                out[i, z] = held[slot] * weight_inverse[i]


def run(kernel, outs, args, scalars=0, scratch=()):
    specs = [pl.BlockSpec(memory_space=pltpu.SMEM)] * scalars
    specs += [pl.BlockSpec(memory_space=pltpu.VMEM)] * (len(args) - scalars)
    shapes = [jax.ShapeDtypeStruct(s, F32) for s in outs]
    return pl.pallas_call(
        kernel,
        out_shape=shapes,
        in_specs=specs,
        out_specs=[pl.BlockSpec(memory_space=pltpu.VMEM)] * len(outs),
        scratch_shapes=[pltpu.VMEM(s, F32) for s in scratch],
        compiler_params=pltpu.CompilerParams(vmem_limit_bytes=32 * 1024 * 1024),
    )(*args)


def neighbours(value_up, value_down, axis):
    peers = lax.axis_size(axis)
    up = [(i, (i + 1) % peers) for i in range(peers)]
    down = [(j, i) for i, j in up]
    return lax.ppermute(value_up, axis, up), lax.ppermute(value_down, axis, down)


def body(pops, codes, offsets, fractions):
    tile = (8, 128)
    (edges,) = run(edge_kernel, [(5,) + tile], (pops, codes))
    left, right = neighbours(edges, edges, "gy")
    p1, wrapped, middle, ahead, behind = run(
        main_kernel,
        [(19, 8) + tile, (10,) + tile, (6, 6) + tile, (4,) + tile, (4,) + tile],
        (pops, codes),
    )
    chunks, post_side, side = run(
        edge_kernel_2,
        [(8, 10) + tile, (20,) + tile, (20,) + tile],
        (left, right, p1, codes, wrapped, middle, ahead, behind),
    )
    own = lax.all_to_all(chunks, "gx", 0, 0)
    below, above = neighbours(own[:, 0:3], own[:, 3:6], "gz")
    p2, ahead, behind = run(
        inner_kernel,
        [(19, 6) + tile, (4,) + tile, (4,) + tile],
        (p1, post_side, side, codes, own),
    )
    (spread,) = run(spread_kernel, [(20, 64, 128)], (own,))
    (planes,) = run(
        plane_kernel,
        [(8, 9) + tile],
        (offsets, fractions, spread, below, above, ahead, behind),
        scalars=2,
        scratch=[(20, 64, 128), (19, 64, 128)],
    )
    planes = lax.all_to_all(planes, "gx", 0, 0)
    (out,) = run(last_kernel, [(19, 8) + tile], (p2, planes))
    return out


def solution(mesh):
    in_specs = (P(None, "gz", "gx", "gy"), P("gz", "gx", "gy"), P(), P())
    out_specs = P(None, "gz", "gx", "gy")
    return jax.shard_map(body, mesh=mesh, in_specs=in_specs, out_specs=out_specs, check_vma=False)
```

```python
import jax
import jax.numpy as jnp
from jax import lax
from jax.experimental import pallas as pl
from jax.experimental.pallas import tpu as pltpu
from jax.sharding import PartitionSpec as P

LEVELS = 8
FRAC_DEN = 64
velocities = (
    (0, 0, 0), (1, 0, 0), (-1, 0, 0), (0, 1, 0), (0, -1, 0), (0, 0, 1), (0, 0, -1),
    (1, 1, 0), (-1, -1, 0), (1, -1, 0), (-1, 1, 0), (1, 0, 1), (-1, 0, -1), (1, 0, -1),
    (-1, 0, 1), (0, 1, 1), (0, -1, -1), (0, 1, -1), (0, -1, 1),
)
weight_inverse = (3.0,) + (18.0,) * 6 + (36.0,) * 12
lattice_weights = tuple(1.0 / v for v in weight_inverse)
relax_time = 0.9
pairs = ((1, 2), (3, 4), (5, 6), (7, 8), (9, 10), (11, 12), (13, 14), (15, 16), (17, 18))
rising = (5, 11, 14, 15, 18)
sinking = (6, 13, 12, 17, 16)
level = (0, 1, 2, 3, 4, 7, 8, 9, 10)
forward = (1, 7, 9, 11, 13)
backward = (2, 8, 10, 12, 14)
sideways = (3, 4, 7, 8, 9, 10, 15, 16, 17, 18)
F32 = jnp.float32


def roll(value, by, axis):
    if isinstance(by, int):
        by %= value.shape[axis]
        if by == 0:
            return value
    return pltpu.roll(value, by, axis)


def lanes(shape=(8, 128)):
    return lax.broadcasted_iota(jnp.int32, shape, 1)


def rows(shape=(8, 128)):
    return lax.broadcasted_iota(jnp.int32, shape, 0)


def collide(f, solid):
    density = f[0]
    for i, j in pairs:
        density = density + (f[i] + f[j])
    inverse = 1.0 / density
    speed = []
    for axis in range(3):
        total = None
        for i, j in pairs:
            moving = velocities[i][axis]
            if moving == 0:
                continue
            part = f[i] - f[j] if moving == 1 else f[j] - f[i]
            total = part if total is None else total + part
        speed.append(total * inverse)
    square = speed[0] * speed[0] + speed[1] * speed[1] + speed[2] * speed[2]
    fluid = 1.0 - solid
    keep = fluid * (1.0 - 1.0 / relax_time)
    pull = fluid * density * (1.0 / relax_time)
    calm = pull - 1.5 * square * pull
    post = [None] * 19
    post[0] = keep * f[0] + lattice_weights[0] * calm + solid * f[0]
    for i, j in pairs:
        along = None
        for axis in range(3):
            moving = velocities[i][axis]
            if moving == 0:
                continue
            if along is None:
                along = speed[axis] if moving == 1 else -speed[axis]
            else:
                along = along + speed[axis] if moving == 1 else along - speed[axis]
        weight = lattice_weights[i]
        flow = (3.0 * weight) * (pull * along)
        even = weight * calm + (1.5 * flow) * along
        post[i] = keep * f[i] + solid * f[j] + (even + flow)
        post[j] = keep * f[j] + solid * f[i] + (even - flow)
    return post


def edge_kernel(pops_far, codes_far, out, pops, codes, sems):
    lane = lanes()
    copies = [pltpu.make_async_copy(pops_far.at[i], pops.at[i], sems.at[i]) for i in range(19)]
    copies.append(pltpu.make_async_copy(codes_far, codes, sems.at[19]))
    for copy in copies:
        copy.start()
    for tile in range(5):
        packed = jnp.zeros((8, 128), F32)
        for slot in range(4):
            item = tile * 4 + slot
            copies[item].wait()
            for z in range(8):
                start = slot * 32 + z * 4
                source = pops[item, z] if item < 19 else codes[z].astype(F32)
                moved = roll(source, start + 2, 1)
                packed = jnp.where(lane < start, packed, moved)
        out[tile] = packed


UPPER = [(i, 7) for i in rising] + [(i, 7) for i in level] + [(i, 6) for i in rising] + [(19, 7)]
LOWER = [(i, 0) for i in sinking] + [(i, 0) for i in level] + [(i, 1) for i in sinking] + [(19, 0)]
NEAR = [(group, tile, slot, i, z) for group, items in enumerate((UPPER, LOWER)) for tile in range(3) for slot, (i, z) in enumerate(items[7 * tile : 7 * tile + 7])]
AHEAD_ROW, BEHIND_ROW = slice(7, 8), slice(0, 1)


def row_place(j, z):
    r = 6 * j + z - 1
    return r // 8, slice(r % 8, r % 8 + 1)


def main_kernel(pops, codes, p1, wrapped, chunks, ahead, behind):
    lane = lanes()
    side = [jnp.zeros((8, 128), F32) for _ in range(19)]
    for z in range(8):
        f = [pops[i, z] * lattice_weights[i] for i in range(19)]
        post = collide(f, codes[z] * (1.0 / LEVELS))
        for i in range(19):
            step = velocities[i][1]
            value = roll(post[i], step, 1)
            if step == 1:
                side[i] = jnp.where(lane == 4 * z + 2, roll(value, 4 * z + 2, 1), side[i])
            elif step == -1:
                side[i] = jnp.where(lane == 4 * z + 1, roll(value, 4 * z + 2, 1), side[i])
            p1[i, z] = value
            target = z + velocities[i][2]
            if 1 <= target <= 6 and i in forward:
                tile, at = row_place(forward.index(i), target)
                ahead[tile, at, :] = value[AHEAD_ROW, :]
            if 1 <= target <= 6 and i in backward:
                tile, at = row_place(backward.index(i), target)
                behind[tile, at, :] = value[BEHIND_ROW, :]
    for k, i in enumerate(sideways):
        wrapped[k] = side[i]
    for group in range(2):
        for tile in range(3):
            held = [jnp.zeros((8, 128), F32)] * 6
            for _, _, slot, i, z in [n for n in NEAR if n[:2] == (group, tile)]:
                source = p1[i, z] if i < 19 else codes[z]
                for d in range(1, 7):
                    moved = roll(source, 18 * slot - 16 * d + 1, 1)
                    held[d - 1] = jnp.where(lane < 18 * slot, held[d - 1], moved)
            for d in range(6):
                chunks[d, group * 3 + tile] = held[d]


def edge_kernel_2(left, right, p1, codes, wrapped, middle, ahead, behind, chunks, post_side, side):
    lane = lanes()
    ends = (lane == 0) | (lane == 127)
    me, peers = lax.axis_index("gx"), lax.axis_size("gx")
    after, before = (me + 1) % peers, (me + peers - 1) % peers
    for tile in range(4):
        chunks[after, 6 + tile] = ahead[tile]
        chunks[before, 6 + tile] = behind[tile]
    for d in range(1, 7):
        for tile in range(6):
            chunks[d, tile] = middle[d - 1, tile]
    outer = []
    for tile in range(5):
        both = jnp.where(lane % 4 < 2, left[tile], right[tile])
        for slot in range(4):
            outer.append(roll(both, -32 * slot, 1))
    beside = collide([outer[i] * lattice_weights[i] for i in range(19)], outer[19] * (1.0 / LEVELS))
    beside.append(outer[19])
    shifted = list(beside)
    for k, i in enumerate(sideways):
        step = velocities[i][1]
        shifted[i] = jnp.where(lane % 4 == (2 if step == 1 else 1), wrapped[k], roll(beside[i], step, 1))
    for i in range(20):
        side[i] = shifted[i]
        post_side[i] = beside[i]
    row_lane = lanes((1, 128))
    for members, to, source, at_x in ((forward, after, ahead, AHEAD_ROW), (backward, before, behind, BEHIND_ROW)):
        extra = [jnp.zeros((1, 128), F32)] * 2
        for j, i in enumerate(members):
            extra[j // 4] = jnp.where(row_lane // 32 == j % 4, roll(shifted[i][at_x, :], 32 * (j % 4), 1), extra[j // 4])
            step = velocities[i][1]
            if step == 0:
                continue
            for z in range(1, 7):
                tile, at = row_place(j, z)
                lane_at, start = (0, 4 * z + 1) if step == 1 else (127, 4 * z + 2)
                fixed = roll(beside[i][at_x, :], lane_at - start, 1)
                chunks[to, 6 + tile, at, :] = jnp.where(row_lane == lane_at, fixed, source[tile, at, :])
        chunks[to, 9, 6:7, :] = extra[0]
        chunks[to, 9, 7:8, :] = extra[1]
    for group in range(2):
        for tile in range(3):
            held = [jnp.zeros((8, 128), F32)] * 2
            for _, _, slot, i, z in [n for n in NEAR if n[:2] == (group, tile)]:
                main = p1[i, z] if i < 19 else codes[z]
                step = velocities[i][1] if i < 19 else 0
                first = last = main
                if step == 1:
                    first = jnp.where(ends, roll(beside[i], 127 - 4 * z, 1), main)
                elif step == -1:
                    last = jnp.where(ends, roll(beside[i], 125 - 4 * z, 1), main)
                else:
                    first = jnp.where(lane == 127, roll(beside[i], 126 - 4 * z, 1), main)
                    last = jnp.where(lane == 0, roll(beside[i], -(4 * z + 2), 1), main)
                held[0] = jnp.where(lane < 18 * slot, held[0], roll(first, 18 * slot + 1, 1))
                held[1] = jnp.where(lane < 18 * slot, held[1], roll(last, 18 * slot - 111, 1))
            chunks[0, group * 3 + tile] = held[0]
            chunks[7, group * 3 + tile] = held[1]


def cross(outgoing, lane, shift_a, shift_b, frac_a, frac_b):
    length = outgoing.shape[0]
    low = (lane // 32) % 2 == 1
    up_a, down_a = roll(outgoing, shift_a, 0), roll(outgoing, (length - shift_a) % length, 0)
    up_b, down_b = roll(outgoing, shift_b, 0), roll(outgoing, (length - shift_b) % length, 0)
    near = jnp.where(lane < 64, jnp.where(low, down_a, up_a), jnp.where(low, down_b, up_b))
    far = jnp.where(low, roll(near, -1, 0), roll(near, 1, 0))
    share = jnp.where(lane < 64, frac_a, frac_b)
    mixed = (1.0 - share) * near + share * far
    return jnp.where(low, roll(mixed, 32, 1), roll(mixed, -32, 1))


def spread_kernel(offsets, fractions, own, work):
    lane8 = lanes()
    for item in range(20):
        tile, slot = divmod(item, 7)
        for b in range(8):
            value = jnp.where(
                lane8 < 64,
                roll(own[b, 3 + tile], 32 - 18 * slot, 1),
                roll(own[b, tile], 64 - 18 * slot, 1),
            )
            work[item, 8 * b : 8 * b + 8, :] = value


def plane_kernel(offsets, fractions, spread, near, far, ahead, behind, out, work, state):
    length = work.shape[1]
    lane8 = lanes()
    lane = lanes((length, 128))
    here = lax.axis_index("gz")
    even = here % 2 == 0
    after = (here + 1) % lax.axis_size("gz")
    me, peers = lax.axis_index("gx"), lax.axis_size("gx")
    for tile in range(4):
        out[(me + 1) % peers, 5 + tile] = ahead[tile]
        out[(me + peers - 1) % peers, 5 + tile] = behind[tile]

    def params(step):
        return (
            offsets[step, here],
            offsets[step, after],
            fractions[step, here].astype(F32) * (1.0 / FRAC_DEN),
            fractions[step, after].astype(F32) * (1.0 / FRAC_DEN),
        )

    for item in range(20):
        tile, slot = divmod(item, 7)
        for b in range(8):
            at = slice(8 * b, 8 * b + 8)
            below = jnp.where(even, far[b, tile], near[b, tile])
            above = jnp.where(even, near[b, tile], far[b, tile])
            moved = jnp.where(
                lane8 < 64,
                roll(below, -18 * slot, 1),
                roll(above, 96 - 18 * slot, 1),
            )
            work[item, at, :] = jnp.where((lane8 >= 32) & (lane8 < 96), spread[item, at, :], moved)
    for j in range(5):
        step_x = velocities[rising[j]][0]
        state[sinking[j]] = roll(cross(work[j], lane, *params(0)), step_x, 0)
        state[rising[j]] = roll(work[14 + j], step_x, 0)
    for k, i in enumerate(level):
        state[i] = roll(work[5 + k], velocities[i][0], 0)
    for b in range(8):
        at = slice(8 * b, 8 * b + 8)
        post = collide([state[i, at, :] for i in range(19)], work[19, at, :] * (1.0 / LEVELS))
        for i in range(19):
            state[i, at, :] = roll(post[i], velocities[i][1], 1)
    final = []
    for i in level:
        final.append((i, None))
    for j in range(5):
        final.append((sinking[j], None))
    for j in range(5):
        final.append((rising[j], j))
    for n, (i, crossing) in enumerate(final):
        value = state[i]
        if crossing is not None:
            value = cross(value, lane, *params(1))
        work[n] = roll(value, velocities[i][0], 0)
    for b in range(8):
        for tile in range(5):
            packed = jnp.zeros((8, 128), F32)
            for slot in range(8):
                n = tile * 8 + slot
                if n >= 38:
                    break
                group, q = (n, 2) if n < 19 else (n - 19, 1)
                moved = roll(work[group, 8 * b : 8 * b + 8, :], 16 * slot - 32 * q - 1, 1)
                packed = jnp.where(lane8 < 16 * slot, packed, moved)
            out[b, tile] = packed


def moved_x(value, i, z, rows_behind, rows_ahead, first_tile, row):
    if i in forward:
        tile, at = row_place(forward.index(i), z)
        source, to = rows_behind(first_tile + tile, at), 0
    elif i in backward:
        tile, at = row_place(backward.index(i), z)
        source, to = rows_ahead(first_tile + tile, at), 7
    else:
        return value
    return jnp.where(row == to, jnp.broadcast_to(source, (8, 128)), roll(value, velocities[i][0], 0))


def inner_kernel(p1, post_side, side, codes, own, p2, ahead, behind):
    lane, row = lanes(), rows()
    me, peers = lax.axis_index("gx"), lax.axis_size("gx")
    after, before = (me + 1) % peers, (me + peers - 1) % peers

    def rows_behind(tile, at):
        return own[before, tile, at, :]

    def rows_ahead(tile, at):
        return own[after, tile, at, :]

    f = []
    for i in range(19):
        value = side[i]
        for members, get, to in ((forward, rows_behind, 0), (backward, rows_ahead, 7)):
            if i in members:
                j = members.index(i)
                source = roll(get(9, slice(6 + j // 4, 7 + j // 4)), -32 * (j % 4), 1)
                value = jnp.where(row == to, jnp.broadcast_to(source, (8, 128)), roll(value, velocities[i][0], 0))
        f.append(roll(value, 4 * velocities[i][2], 1))
    beside = collide(f, side[19] * (1.0 / LEVELS))
    for j in range(2):
        ahead[3, 6 + j : 7 + j, :] = jnp.zeros((1, 128), F32)
        behind[3, 6 + j : 7 + j, :] = jnp.zeros((1, 128), F32)

    def mended(value, edge, step, z):
        if step == 1:
            return jnp.where(lane == 0, roll(edge, -(4 * z + 1), 1), value)
        if step == -1:
            return jnp.where(lane == 127, roll(edge, 127 - (4 * z + 2), 1), value)
        return value

    for z in range(1, 7):
        f = []
        for i in range(19):
            source = z - velocities[i][2]
            value = mended(p1[i, source], post_side[i], velocities[i][1], source)
            f.append(moved_x(value, i, z, rows_behind, rows_ahead, 6, row))
        post = collide(f, codes[z] * (1.0 / LEVELS))
        for i in range(19):
            step = velocities[i][1]
            value = mended(roll(post[i], step, 1), beside[i], step, z)
            p2[i, z - 1] = value
            if i in forward:
                tile, at = row_place(forward.index(i), z)
                ahead[tile, at, :] = value[AHEAD_ROW, :]
            if i in backward:
                tile, at = row_place(backward.index(i), z)
                behind[tile, at, :] = value[BEHIND_ROW, :]


def last_kernel(p2, planes, out, held_out, sems):
    lane, row = lanes(), rows()
    me, peers = lax.axis_index("gx"), lax.axis_size("gx")
    after, before = (me + 1) % peers, (me + peers - 1) % peers

    def rows_behind(tile, at):
        return planes[before, tile, at, :]

    def rows_ahead(tile, at):
        return planes[after, tile, at, :]

    target = []
    for group in range(2):
        z, inner = (7, 6) if group == 0 else (0, 1)
        inward, outward = (sinking, rising) if group == 0 else (rising, sinking)
        target += [(i, z) for i in level] + [(i, inner) for i in inward] + [(i, z) for i in inward]
    part = lane // 16
    for tile in range(5):
        held = [planes[h, tile] for h in range(8)]
        for k in (1, 2, 4):
            fixed = part & k == 0
            for h in range(8):
                if h & k == 0:
                    lo, hi = held[h], held[h | k]
                    held[h] = jnp.where(fixed, lo, roll(hi, 16 * k, 1))
                    held[h | k] = jnp.where(fixed, roll(lo, -16 * k, 1), hi)
        for slot in range(8):
            n = tile * 8 + slot
            if n < 38:
                i, z = target[n]
                held_out[i, z] = held[slot] * weight_inverse[i]
    copies = []
    for i in range(19):
        for z in range(8):
            source = z - velocities[i][2]
            if 1 <= source <= 6:
                value = moved_x(p2[i, source - 1], i, source, rows_behind, rows_ahead, 5, row)
                held_out[i, z] = value * weight_inverse[i]
        copies.append(pltpu.make_async_copy(held_out.at[i], out.at[i], sems.at[i]))
        copies[i].start()
    for copy in copies:
        copy.wait()


def run(kernel, outs, args, scalars=0, scratch=(), far_in=False, far_out=False, sems=0):
    near = pl.BlockSpec(memory_space=pltpu.VMEM)
    away = pl.BlockSpec(memory_space=pltpu.HBM)
    specs = [pl.BlockSpec(memory_space=pltpu.SMEM)] * scalars
    specs += [away if far_in else near] * (len(args) - scalars)
    shapes = [jax.ShapeDtypeStruct(s, F32) for s in outs]

    def held(s):
        return pltpu.VMEM(s.shape, s.dtype) if isinstance(s, jax.ShapeDtypeStruct) else pltpu.VMEM(s, F32)

    return pl.pallas_call(
        kernel,
        out_shape=shapes,
        in_specs=specs,
        out_specs=[away if far_out else near] * len(outs),
        scratch_shapes=[held(s) for s in scratch] + [pltpu.SemaphoreType.DMA((sems,))] * (sems > 0),
        compiler_params=pltpu.CompilerParams(vmem_limit_bytes=32 * 1024 * 1024),
    )(*args)


def neighbours(value_up, value_down, axis):
    peers = lax.axis_size(axis)
    up = [(i, (i + 1) % peers) for i in range(peers)]
    down = [(j, i) for i, j in up]
    return lax.ppermute(value_up, axis, up), lax.ppermute(value_down, axis, down)


def swaps(own):
    peers = lax.axis_size("gz")
    even = lax.axis_index("gz") % 2 == 0
    upper, lower = own[:, 0:3], own[:, 3:6]
    pair = [(i, i ^ 1) for i in range(peers)]
    other = [(i, (i + peers - 1) % peers if i % 2 == 0 else (i + 1) % peers) for i in range(peers)]
    far = lax.ppermute(jnp.where(even, lower, upper), "gz", other)
    near = lax.ppermute(jnp.where(even, upper, lower), "gz", pair)
    return near, far


def body(pops, codes, offsets, fractions):
    tile = (8, 128)
    far = [pltpu.with_memory_space_constraint(value, pltpu.HBM) for value in (pops, codes)]
    (edges,) = run(
        edge_kernel,
        [(5,) + tile],
        far,
        scratch=[(19, 8) + tile, jax.ShapeDtypeStruct((8,) + tile, jnp.int32)],
        far_in=True,
        sems=20,
    )
    codes = codes.astype(F32)
    left, right = neighbours(edges, edges, "gy")
    p1, wrapped, middle, ahead, behind = run(
        main_kernel,
        [(19, 8) + tile, (10,) + tile, (6, 6) + tile, (4,) + tile, (4,) + tile],
        (pops, codes),
    )
    chunks, post_side, side = run(
        edge_kernel_2,
        [(8, 10) + tile, (20,) + tile, (20,) + tile],
        (left, right, p1, codes, wrapped, middle, ahead, behind),
    )
    own = lax.all_to_all(chunks, "gx", 0, 0)
    near, far = swaps(own)
    p2, ahead, behind = run(
        inner_kernel,
        [(19, 6) + tile, (4,) + tile, (4,) + tile],
        (p1, post_side, side, codes, own),
    )
    (spread,) = run(spread_kernel, [(20, 64, 128)], (offsets, fractions, own), scalars=2)
    (planes,) = run(
        plane_kernel,
        [(8, 9) + tile],
        (offsets, fractions, spread, near, far, ahead, behind),
        scalars=2,
        scratch=[(20, 64, 128), (19, 64, 128)],
    )
    planes = lax.all_to_all(planes, "gx", 0, 0)
    (out,) = run(
        last_kernel, [(19, 8) + tile], (p2, planes), scratch=[(19, 8) + tile], far_out=True, sems=19
    )
    return out


def solution(mesh):
    in_specs = (P(None, "gz", "gx", "gy"), P("gz", "gx", "gy"), P(), P())
    out_specs = P(None, "gz", "gx", "gy")
    return jax.shard_map(body, mesh=mesh, in_specs=in_specs, out_specs=out_specs, check_vma=False)
```

```python
import jax
import jax.numpy as jnp
from jax import lax
from jax.experimental import pallas as pl
from jax.experimental.pallas import tpu as pltpu
from jax.sharding import PartitionSpec as P

LEVELS = 8
FRAC_DEN = 64
velocities = (
    (0, 0, 0), (1, 0, 0), (-1, 0, 0), (0, 1, 0), (0, -1, 0), (0, 0, 1), (0, 0, -1),
    (1, 1, 0), (-1, -1, 0), (1, -1, 0), (-1, 1, 0), (1, 0, 1), (-1, 0, -1), (1, 0, -1),
    (-1, 0, 1), (0, 1, 1), (0, -1, -1), (0, 1, -1), (0, -1, 1),
)
weight_inverse = (3.0,) + (18.0,) * 6 + (36.0,) * 12
lattice_weights = tuple(1.0 / v for v in weight_inverse)
relax_time = 0.9
pairs = ((1, 2), (3, 4), (5, 6), (7, 8), (9, 10), (11, 12), (13, 14), (15, 16), (17, 18))
rising = (5, 11, 14, 15, 18)
sinking = (6, 13, 12, 17, 16)
level = (0, 1, 2, 3, 4, 7, 8, 9, 10)
forward = (1, 7, 9, 11, 13)
backward = (2, 8, 10, 12, 14)
sideways = (3, 4, 7, 8, 9, 10, 15, 16, 17, 18)
F32 = jnp.float32


def roll(value, by, axis):
    if isinstance(by, int):
        by %= value.shape[axis]
        if by == 0:
            return value
    return pltpu.roll(value, by, axis)


def lanes(shape=(8, 128)):
    return lax.broadcasted_iota(jnp.int32, shape, 1)


def rows(shape=(8, 128)):
    return lax.broadcasted_iota(jnp.int32, shape, 0)


def collide(f, solid):
    density = f[0]
    for i, j in pairs:
        density = density + (f[i] + f[j])
    inverse = 1.0 / density
    speed = []
    for axis in range(3):
        total = None
        for i, j in pairs:
            moving = velocities[i][axis]
            if moving == 0:
                continue
            part = f[i] - f[j] if moving == 1 else f[j] - f[i]
            total = part if total is None else total + part
        speed.append(total * inverse)
    square = speed[0] * speed[0] + speed[1] * speed[1] + speed[2] * speed[2]
    fluid = 1.0 - solid
    keep = fluid * (1.0 - 1.0 / relax_time)
    pull = fluid * density * (1.0 / relax_time)
    calm = pull - 1.5 * square * pull
    post = [None] * 19
    post[0] = keep * f[0] + lattice_weights[0] * calm + solid * f[0]
    for i, j in pairs:
        along = None
        for axis in range(3):
            moving = velocities[i][axis]
            if moving == 0:
                continue
            if along is None:
                along = speed[axis] if moving == 1 else -speed[axis]
            else:
                along = along + speed[axis] if moving == 1 else along - speed[axis]
        weight = lattice_weights[i]
        flow = (3.0 * weight) * (pull * along)
        even = weight * calm + (1.5 * flow) * along
        post[i] = keep * f[i] + solid * f[j] + (even + flow)
        post[j] = keep * f[j] + solid * f[i] + (even - flow)
    return post


def edge_kernel(pops_far, codes_far, out, pops, codes, sems):
    lane = lanes()
    copies = []
    for tile in range(5):
        part = pl.ds(4 * tile, min(4, 19 - 4 * tile))
        copies.append(pltpu.make_async_copy(pops_far.at[part], pops.at[part], sems.at[tile]))
    copies.append(pltpu.make_async_copy(codes_far, codes, sems.at[5]))
    for copy in copies:
        copy.start()
    for tile in range(5):
        copies[tile].wait()
        packed = jnp.zeros((8, 128), F32)
        for slot in range(4):
            item = tile * 4 + slot
            if item == 19:
                copies[5].wait()
            for z in range(8):
                start = slot * 32 + z * 4
                source = pops[item, z] if item < 19 else codes[z].astype(F32)
                moved = roll(source, start + 2, 1)
                packed = jnp.where(lane < start, packed, moved)
        out[tile] = packed


UPPER = [(i, 7) for i in rising] + [(i, 7) for i in level] + [(i, 6) for i in rising] + [(19, 7)]
LOWER = [(i, 0) for i in sinking] + [(i, 0) for i in level] + [(i, 1) for i in sinking] + [(19, 0)]
NEAR = [(group, tile, slot, i, z) for group, items in enumerate((UPPER, LOWER)) for tile in range(3) for slot, (i, z) in enumerate(items[7 * tile : 7 * tile + 7])]
AHEAD_ROW, BEHIND_ROW = slice(7, 8), slice(0, 1)


def set_bases():
    odd = lax.axis_index("gz") % 2
    return 3 * odd, 3 - 3 * odd


def row_place(j, z):
    r = 6 * j + z - 1
    return r // 8, slice(r % 8, r % 8 + 1)


def main_kernel(pops, codes, p1, wrapped, chunks, ahead, behind):
    lane = lanes()
    side = [jnp.zeros((8, 128), F32) for _ in range(19)]
    for z in range(8):
        f = [pops[i, z] * lattice_weights[i] for i in range(19)]
        post = collide(f, codes[z].astype(F32) * (1.0 / LEVELS))
        for i in range(19):
            step = velocities[i][1]
            value = roll(post[i], step, 1)
            if step == 1:
                side[i] = jnp.where(lane == 4 * z + 2, roll(value, 4 * z + 2, 1), side[i])
            elif step == -1:
                side[i] = jnp.where(lane == 4 * z + 1, roll(value, 4 * z + 2, 1), side[i])
            p1[i, z] = value
            target = z + velocities[i][2]
            if 1 <= target <= 6 and i in forward:
                tile, at = row_place(forward.index(i), target)
                ahead[tile, at, :] = value[AHEAD_ROW, :]
            if 1 <= target <= 6 and i in backward:
                tile, at = row_place(backward.index(i), target)
                behind[tile, at, :] = value[BEHIND_ROW, :]
    for k, i in enumerate(sideways):
        wrapped[k] = side[i]
    for group in range(2):
        for tile in range(3):
            held = [jnp.zeros((8, 128), F32)] * 6
            place = (lane + 32 * group) % 128
            for _, _, slot, i, z in [n for n in NEAR if n[:2] == (group, tile)]:
                source = p1[i, z] if i < 19 else codes[z].astype(F32)
                for d in range(1, 7):
                    moved = roll(source, 18 * slot - 16 * d + 1 + 96 * group, 1)
                    held[d - 1] = jnp.where(place < 18 * slot, held[d - 1], moved)
            for d in range(6):
                chunks[d, group * 3 + tile] = held[d]


def edge_kernel_2(left, right, p1, codes, wrapped, middle, ahead, behind, chunks, post_side, side):
    lane = lanes()
    ends = (lane == 0) | (lane == 127)
    me, peers = lax.axis_index("gx"), lax.axis_size("gx")
    after, before = (me + 1) % peers, (me + peers - 1) % peers
    for tile in range(4):
        chunks[after, 6 + tile] = ahead[tile]
        chunks[before, 6 + tile] = behind[tile]
    bases = set_bases()
    for d in range(1, 7):
        for tile in range(3):
            chunks[d, bases[0] + tile] = middle[d - 1, tile]
            chunks[d, bases[1] + tile] = middle[d - 1, 3 + tile]
    outer = []
    for tile in range(5):
        both = jnp.where(lane % 4 < 2, left[tile], right[tile])
        for slot in range(4):
            outer.append(roll(both, -32 * slot, 1))
    beside = collide([outer[i] * lattice_weights[i] for i in range(19)], outer[19] * (1.0 / LEVELS))
    beside.append(outer[19])
    shifted = list(beside)
    for k, i in enumerate(sideways):
        step = velocities[i][1]
        shifted[i] = jnp.where(lane % 4 == (2 if step == 1 else 1), wrapped[k], roll(beside[i], step, 1))
    for i in range(20):
        side[i] = shifted[i]
        post_side[i] = beside[i]
    row_lane = lanes((1, 128))
    for members, to, source, at_x in ((forward, after, ahead, AHEAD_ROW), (backward, before, behind, BEHIND_ROW)):
        extra = [jnp.zeros((1, 128), F32)] * 2
        for j, i in enumerate(members):
            extra[j // 4] = jnp.where(row_lane // 32 == j % 4, roll(shifted[i][at_x, :], 32 * (j % 4), 1), extra[j // 4])
            step = velocities[i][1]
            if step == 0:
                continue
            for z in range(1, 7):
                tile, at = row_place(j, z)
                lane_at, start = (0, 4 * z + 1) if step == 1 else (127, 4 * z + 2)
                fixed = roll(beside[i][at_x, :], lane_at - start, 1)
                chunks[to, 6 + tile, at, :] = jnp.where(row_lane == lane_at, fixed, source[tile, at, :])
        chunks[to, 9, 6:7, :] = extra[0]
        chunks[to, 9, 7:8, :] = extra[1]
    for group in range(2):
        for tile in range(3):
            held = [jnp.zeros((8, 128), F32)] * 2
            place, shift = (lane + 32 * group) % 128, 96 * group
            for _, _, slot, i, z in [n for n in NEAR if n[:2] == (group, tile)]:
                main = p1[i, z] if i < 19 else codes[z].astype(F32)
                step = velocities[i][1] if i < 19 else 0
                first = last = main
                if step == 1:
                    first = jnp.where(ends, roll(beside[i], 127 - 4 * z, 1), main)
                elif step == -1:
                    last = jnp.where(ends, roll(beside[i], 125 - 4 * z, 1), main)
                else:
                    first = jnp.where(lane == 127, roll(beside[i], 126 - 4 * z, 1), main)
                    last = jnp.where(lane == 0, roll(beside[i], -(4 * z + 2), 1), main)
                held[0] = jnp.where(place < 18 * slot, held[0], roll(first, 18 * slot + 1 + shift, 1))
                held[1] = jnp.where(place < 18 * slot, held[1], roll(last, 18 * slot - 111 + shift, 1))
            chunks[0, bases[group] + tile] = held[0]
            chunks[7, bases[group] + tile] = held[1]


def cross(outgoing, lane, shift_a, shift_b, frac_a, frac_b):
    length = outgoing.shape[0]
    low = (lane // 32) % 2 == 1
    up_a, down_a = roll(outgoing, shift_a, 0), roll(outgoing, (length - shift_a) % length, 0)
    up_b, down_b = roll(outgoing, shift_b, 0), roll(outgoing, (length - shift_b) % length, 0)
    near = jnp.where(lane < 64, jnp.where(low, down_a, up_a), jnp.where(low, down_b, up_b))
    far = jnp.where(low, roll(near, -1, 0), roll(near, 1, 0))
    share = jnp.where(lane < 64, frac_a, frac_b)
    mixed = (1.0 - share) * near + share * far
    return jnp.where(low, roll(mixed, 32, 1), roll(mixed, -32, 1))


def spread_kernel(own, work):
    lane8 = lanes()
    upper, lower = set_bases()
    for item in range(20):
        tile, slot = divmod(item, 7)
        to = (64 - 18 * slot) % 128
        mine = (lane8 + to) % 128 >= 64
        for b in range(8):
            value = jnp.where(mine, own[b, upper + tile], own[b, lower + tile])
            work[item, 8 * b : 8 * b + 8, :] = roll(value, to, 1)


def plane_kernel(offsets_far, fractions_far, spread, near, far, ahead, behind, out, work, state, offsets, fractions, sems):
    copies = [
        pltpu.make_async_copy(offsets_far, offsets, sems.at[0]),
        pltpu.make_async_copy(fractions_far, fractions, sems.at[1]),
    ]
    for copy in copies:
        copy.start()
    length = work.shape[1]
    lane8 = lanes()
    lane = lanes((length, 128))
    here = lax.axis_index("gz")
    odd = here % 2
    after = (here + 1) % lax.axis_size("gz")
    me, peers = lax.axis_index("gx"), lax.axis_size("gx")
    for tile in range(4):
        out[(me + 1) % peers, 5 + tile] = ahead[tile]
        out[(me + peers - 1) % peers, 5 + tile] = behind[tile]

    def params(step):
        return (
            offsets[step, here],
            offsets[step, after],
            fractions[step, here].astype(F32) * (1.0 / FRAC_DEN),
            fractions[step, after].astype(F32) * (1.0 / FRAC_DEN),
        )

    for item in range(20):
        tile, slot = divmod(item, 7)
        to = (-18 * slot) % 128
        paired = (lane8 + to + 64 * (1 - odd)) % 128 < 64
        for b in range(8):
            at = slice(8 * b, 8 * b + 8)
            value = roll(jnp.where(paired, near[b, tile], far[b, tile]), to, 1)
            work[item, at, :] = jnp.where((lane8 >= 32) & (lane8 < 96), spread[item, at, :], value)
    for copy in copies:
        copy.wait()
    for j in range(5):
        step_x = velocities[rising[j]][0]
        state[sinking[j]] = roll(cross(work[j], lane, *params(0)), step_x, 0)
        state[rising[j]] = roll(work[14 + j], step_x, 0)
    for k, i in enumerate(level):
        state[i] = roll(work[5 + k], velocities[i][0], 0)
    for b in range(8):
        at = slice(8 * b, 8 * b + 8)
        post = collide([state[i, at, :] for i in range(19)], work[19, at, :] * (1.0 / LEVELS))
        for i in range(19):
            state[i, at, :] = roll(post[i], velocities[i][1], 1)
    final = []
    for i in level:
        final.append((i, None))
    for j in range(5):
        final.append((sinking[j], None))
    for j in range(5):
        final.append((rising[j], j))
    for n, (i, crossing) in enumerate(final):
        value = state[i]
        if crossing is not None:
            value = cross(value, lane, *params(1))
        work[n] = roll(value, velocities[i][0], 0)
    part = lane8 // 16
    for b in range(8):
        for tile in range(5):
            packed = jnp.zeros((8, 128), F32)
            for k in range(4):
                n = tile * 4 + k
                if n >= 19:
                    break
                slot = 4 * (k // 2) + k % 2
                moved = roll(work[n, 8 * b : 8 * b + 8, :], 16 * slot - 33, 1)
                packed = jnp.where((part == slot) | (part == slot + 2), moved, packed)
            out[b, tile] = packed


def moved_x(value, i, z, rows_behind, rows_ahead, first_tile, row):
    if i in forward:
        tile, at = row_place(forward.index(i), z)
        source, to = rows_behind(first_tile + tile, at), 0
    elif i in backward:
        tile, at = row_place(backward.index(i), z)
        source, to = rows_ahead(first_tile + tile, at), 7
    else:
        return value
    return jnp.where(row == to, jnp.broadcast_to(source, (8, 128)), roll(value, velocities[i][0], 0))


def inner_kernel(p1, post_side, side, codes, own, p2, ahead, behind):
    lane, row = lanes(), rows()
    me, peers = lax.axis_index("gx"), lax.axis_size("gx")
    after, before = (me + 1) % peers, (me + peers - 1) % peers

    def rows_behind(tile, at):
        return own[before, tile, at, :]

    def rows_ahead(tile, at):
        return own[after, tile, at, :]

    f = []
    for i in range(19):
        value = side[i]
        for members, get, to in ((forward, rows_behind, 0), (backward, rows_ahead, 7)):
            if i in members:
                j = members.index(i)
                source = roll(get(9, slice(6 + j // 4, 7 + j // 4)), -32 * (j % 4), 1)
                value = jnp.where(row == to, jnp.broadcast_to(source, (8, 128)), roll(value, velocities[i][0], 0))
        f.append(roll(value, 4 * velocities[i][2], 1))
    beside = collide(f, side[19] * (1.0 / LEVELS))
    for j in range(2):
        ahead[3, 6 + j : 7 + j, :] = jnp.zeros((1, 128), F32)
        behind[3, 6 + j : 7 + j, :] = jnp.zeros((1, 128), F32)

    def mended(value, edge, step, z):
        if step == 1:
            return jnp.where(lane == 0, roll(edge, -(4 * z + 1), 1), value)
        if step == -1:
            return jnp.where(lane == 127, roll(edge, 127 - (4 * z + 2), 1), value)
        return value

    for z in range(1, 7):
        f = []
        for i in range(19):
            source = z - velocities[i][2]
            value = mended(p1[i, source], post_side[i], velocities[i][1], source)
            f.append(moved_x(value, i, z, rows_behind, rows_ahead, 6, row))
        post = collide(f, codes[z].astype(F32) * (1.0 / LEVELS))
        for i in range(19):
            step = velocities[i][1]
            value = mended(roll(post[i], step, 1), beside[i], step, z)
            p2[i, z - 1] = value
            if i in forward:
                tile, at = row_place(forward.index(i), z)
                ahead[tile, at, :] = value[AHEAD_ROW, :]
            if i in backward:
                tile, at = row_place(backward.index(i), z)
                behind[tile, at, :] = value[BEHIND_ROW, :]


def last_kernel(p2, planes, out, held_out, sems):
    lane, row = lanes(), rows()
    me, peers = lax.axis_index("gx"), lax.axis_size("gx")
    after, before = (me + 1) % peers, (me + peers - 1) % peers

    def rows_behind(tile, at):
        return planes[before, tile, at, :]

    def rows_ahead(tile, at):
        return planes[after, tile, at, :]

    target = []
    for group in range(2):
        z, inner = (7, 6) if group == 0 else (0, 1)
        inward = sinking if group == 0 else rising
        target.append([(i, z) for i in level] + [(i, inner) for i in inward] + [(i, z) for i in inward])
    part = lane // 16
    for tile in range(5):
        held = [planes[h, tile] for h in range(8)]
        for k in (1, 2, 4):
            fixed = part & k == 0
            for h in range(8):
                if h & k == 0:
                    lo, hi = held[h], held[h | k]
                    held[h] = jnp.where(fixed, lo, roll(hi, 16 * k, 1))
                    held[h | k] = jnp.where(fixed, roll(lo, -16 * k, 1), hi)
        for slot in range(8):
            n = tile * 4 + 2 * (slot // 4) + slot % 2
            if n < 19:
                i, z = target[0 if slot % 4 >= 2 else 1][n]
                held_out[i, z] = held[slot] * weight_inverse[i]
    copies = []
    for i in range(19):
        for z in range(8):
            source = z - velocities[i][2]
            if 1 <= source <= 6:
                value = moved_x(p2[i, source - 1], i, source, rows_behind, rows_ahead, 5, row)
                held_out[i, z] = value * weight_inverse[i]
        if i % 5 == 4 or i == 18:
            start = i - i % 5
            part = pl.ds(start, i + 1 - start)
            copies.append(pltpu.make_async_copy(held_out.at[part], out.at[part], sems.at[i // 5]))
            copies[-1].start()
    for copy in copies:
        copy.wait()


def run(kernel, outs, args, scratch=(), words=(), far_in=0, far_out=False, sems=0):
    near = pl.BlockSpec(memory_space=pltpu.VMEM)
    away = pl.BlockSpec(memory_space=pltpu.HBM)
    return pl.pallas_call(
        kernel,
        out_shape=[s if isinstance(s, jax.ShapeDtypeStruct) else jax.ShapeDtypeStruct(s, F32) for s in outs],
        in_specs=[away] * far_in + [near] * (len(args) - far_in),
        out_specs=[away if far_out else near] * len(outs),
        scratch_shapes=[pltpu.VMEM(s, F32) for s in scratch]
        + [pltpu.SMEM(s, jnp.int32) for s in words]
        + [pltpu.SemaphoreType.DMA((sems,))] * (sems > 0),
        compiler_params=pltpu.CompilerParams(vmem_limit_bytes=32 * 1024 * 1024),
    )(*args)


def neighbours(value_up, value_down, axis):
    peers = lax.axis_size(axis)
    up = [(i, (i + 1) % peers) for i in range(peers)]
    down = [(j, i) for i, j in up]
    return lax.ppermute(value_up, axis, up), lax.ppermute(value_down, axis, down)


def swaps(own):
    peers = lax.axis_size("gz")
    pair = [(i, i ^ 1) for i in range(peers)]
    other = [(i, (i + peers - 1) % peers if i % 2 == 0 else (i + 1) % peers) for i in range(peers)]
    far = lax.ppermute(own[:, 3:6], "gz", other)
    near = lax.ppermute(own[:, 0:3], "gz", pair)
    return near, far


def body(pops, codes, offsets, fractions):
    tile = (8, 128)
    pops, codes, offsets, fractions = (
        pltpu.with_memory_space_constraint(value, pltpu.HBM) for value in (pops, codes, offsets, fractions)
    )
    edges, pops, codes = run(
        edge_kernel,
        [(5,) + tile, (19, 8) + tile, jax.ShapeDtypeStruct((8,) + tile, jnp.int32)],
        (pops, codes),
        far_in=2,
        sems=6,
    )
    left, right = neighbours(edges, edges, "gy")
    p1, wrapped, middle, ahead, behind = run(
        main_kernel,
        [(19, 8) + tile, (10,) + tile, (6, 6) + tile, (4,) + tile, (4,) + tile],
        (pops, codes),
    )
    chunks, post_side, side = run(
        edge_kernel_2,
        [(8, 10) + tile, (20,) + tile, (20,) + tile],
        (left, right, p1, codes, wrapped, middle, ahead, behind),
    )
    own = lax.all_to_all(chunks, "gx", 0, 0)
    near, far = swaps(own)
    p2, ahead, behind = run(
        inner_kernel,
        [(19, 6) + tile, (4,) + tile, (4,) + tile],
        (p1, post_side, side, codes, own),
    )
    (spread,) = run(spread_kernel, [(20, 64, 128)], (own,))
    (planes,) = run(
        plane_kernel,
        [(8, 9) + tile],
        (offsets, fractions, spread, near, far, ahead, behind),
        far_in=2,
        scratch=[(20, 64, 128), (19, 64, 128)],
        words=[offsets.shape] * 2,
        sems=2,
    )
    planes = lax.all_to_all(planes, "gx", 0, 0)
    (out,) = run(
        last_kernel, [(19, 8) + tile], (p2, planes), scratch=[(19, 8) + tile], far_out=True, sems=4
    )
    return out


def solution(mesh):
    in_specs = (P(None, "gz", "gx", "gy"), P("gz", "gx", "gy"), P(), P())
    out_specs = P(None, "gz", "gx", "gy")
    return jax.shard_map(body, mesh=mesh, in_specs=in_specs, out_specs=out_specs, check_vma=False)
```

```python
import jax
import jax.numpy as jnp
from jax import lax
from jax.experimental import pallas as pl
from jax.experimental.pallas import tpu as pltpu
from jax.sharding import PartitionSpec as P

LEVELS = 8
FRAC_DEN = 64
velocities = (
    (0, 0, 0), (1, 0, 0), (-1, 0, 0), (0, 1, 0), (0, -1, 0), (0, 0, 1), (0, 0, -1),
    (1, 1, 0), (-1, -1, 0), (1, -1, 0), (-1, 1, 0), (1, 0, 1), (-1, 0, -1), (1, 0, -1),
    (-1, 0, 1), (0, 1, 1), (0, -1, -1), (0, 1, -1), (0, -1, 1),
)
weight_inverse = (3.0,) + (18.0,) * 6 + (36.0,) * 12
lattice_weights = tuple(1.0 / v for v in weight_inverse)
relax_time = 0.9
pairs = ((1, 2), (3, 4), (5, 6), (7, 8), (9, 10), (11, 12), (13, 14), (15, 16), (17, 18))
rising = (5, 11, 14, 15, 18)
sinking = (6, 13, 12, 17, 16)
level = (0, 1, 2, 3, 4, 7, 8, 9, 10)
forward = (1, 7, 9, 11, 13)
backward = (2, 8, 10, 12, 14)
sideways = (3, 4, 7, 8, 9, 10, 15, 16, 17, 18)
F32 = jnp.float32


def roll(value, by, axis):
    if isinstance(by, int):
        by %= value.shape[axis]
        if by == 0:
            return value
    return pltpu.roll(value, by, axis)


def lanes(shape=(8, 128)):
    return lax.broadcasted_iota(jnp.int32, shape, 1)


def rows(shape=(8, 128)):
    return lax.broadcasted_iota(jnp.int32, shape, 0)


def collide(f, solid):
    density = f[0]
    for i, j in pairs:
        density = density + (f[i] + f[j])
    inverse = 1.0 / density
    speed = []
    for axis in range(3):
        total = None
        for i, j in pairs:
            moving = velocities[i][axis]
            if moving == 0:
                continue
            part = f[i] - f[j] if moving == 1 else f[j] - f[i]
            total = part if total is None else total + part
        speed.append(total * inverse)
    square = speed[0] * speed[0] + speed[1] * speed[1] + speed[2] * speed[2]
    fluid = 1.0 - solid
    keep = fluid * (1.0 - 1.0 / relax_time)
    pull = fluid * density * (1.0 / relax_time)
    calm = pull - 1.5 * square * pull
    post = [None] * 19
    post[0] = keep * f[0] + lattice_weights[0] * calm + solid * f[0]
    for i, j in pairs:
        along = None
        for axis in range(3):
            moving = velocities[i][axis]
            if moving == 0:
                continue
            if along is None:
                along = speed[axis] if moving == 1 else -speed[axis]
            else:
                along = along + speed[axis] if moving == 1 else along - speed[axis]
        weight = lattice_weights[i]
        flow = (3.0 * weight) * (pull * along)
        even = weight * calm + (1.5 * flow) * along
        post[i] = keep * f[i] + solid * f[j] + (even + flow)
        post[j] = keep * f[j] + solid * f[i] + (even - flow)
    return post


def edge_kernel(pops_far, codes_far, out, pops, codes, sems):
    lane = lanes()
    copies = []
    for tile in range(5):
        part = pl.ds(4 * tile, min(4, 19 - 4 * tile))
        copies.append(pltpu.make_async_copy(pops_far.at[part], pops.at[part], sems.at[tile]))
    copies.append(pltpu.make_async_copy(codes_far, codes, sems.at[5]))
    for copy in copies:
        copy.start()
    for tile in range(5):
        copies[tile].wait()
        packed = jnp.zeros((8, 128), F32)
        for slot in range(4):
            item = tile * 4 + slot
            if item == 19:
                copies[5].wait()
            for z in range(8):
                start = slot * 32 + z * 4
                source = pops[item, z] if item < 19 else codes[z].astype(F32)
                moved = roll(source, start + 2, 1)
                packed = jnp.where(lane < start, packed, moved)
        out[tile] = packed


UPPER = [(i, 7) for i in rising] + [(i, 7) for i in level] + [(i, 6) for i in rising] + [(19, 7)]
LOWER = [(i, 0) for i in sinking] + [(i, 0) for i in level] + [(i, 1) for i in sinking] + [(19, 0)]
NEAR = [(group, tile, slot, i, z) for group, items in enumerate((UPPER, LOWER)) for tile in range(3) for slot, (i, z) in enumerate(items[7 * tile : 7 * tile + 7])]
AHEAD_ROW, BEHIND_ROW = slice(7, 8), slice(0, 1)


def set_bases():
    odd = lax.axis_index("gz") % 2
    return 3 * odd, 3 - 3 * odd


def row_place(j, z):
    r = 6 * j + z - 1
    return r // 8, slice(r % 8, r % 8 + 1)


def main_kernel(pops, codes, p1, wrapped, chunks, ahead, behind):
    lane = lanes()
    side = [jnp.zeros((8, 128), F32) for _ in range(19)]
    for z in range(8):
        f = [pops[i, z] * lattice_weights[i] for i in range(19)]
        post = collide(f, codes[z].astype(F32) * (1.0 / LEVELS))
        for i in range(19):
            step = velocities[i][1]
            value = roll(post[i], step, 1)
            if step == 1:
                side[i] = jnp.where(lane == 4 * z + 2, roll(value, 4 * z + 2, 1), side[i])
            elif step == -1:
                side[i] = jnp.where(lane == 4 * z + 1, roll(value, 4 * z + 2, 1), side[i])
            p1[i, z] = value
            target = z + velocities[i][2]
            if 1 <= target <= 6 and i in forward:
                tile, at = row_place(forward.index(i), target)
                ahead[tile, at, :] = value[AHEAD_ROW, :]
            if 1 <= target <= 6 and i in backward:
                tile, at = row_place(backward.index(i), target)
                behind[tile, at, :] = value[BEHIND_ROW, :]
    for k, i in enumerate(sideways):
        wrapped[k] = side[i]
    for group in range(2):
        for tile in range(3):
            held = [jnp.zeros((8, 128), F32)] * 6
            place = (lane + 32 * group) % 128
            for _, _, slot, i, z in [n for n in NEAR if n[:2] == (group, tile)]:
                source = p1[i, z] if i < 19 else codes[z].astype(F32)
                for d in range(1, 7):
                    moved = roll(source, 18 * slot - 16 * d + 1 + 96 * group, 1)
                    held[d - 1] = jnp.where(place < 18 * slot, held[d - 1], moved)
            for d in range(6):
                chunks[d, group * 3 + tile] = held[d]


def edge_kernel_2(near, far, p1, codes, wrapped, middle, ahead, behind, chunks, post_side, side):
    lane = lanes()
    ends = (lane == 0) | (lane == 127)
    me, peers = lax.axis_index("gx"), lax.axis_size("gx")
    after, before = (me + 1) % peers, (me + peers - 1) % peers
    for tile in range(4):
        chunks[after, 6 + tile] = ahead[tile]
        chunks[before, 6 + tile] = behind[tile]
    bases = set_bases()
    for d in range(1, 7):
        for tile in range(3):
            chunks[d, bases[0] + tile] = middle[d - 1, tile]
            chunks[d, bases[1] + tile] = middle[d - 1, 3 + tile]
    outer = []
    paired = (lane // 2 + lax.axis_index("gy")) % 2 == 1
    for tile in range(5):
        both = jnp.where(paired, near[tile], far[tile])
        for slot in range(4):
            outer.append(roll(both, -32 * slot, 1))
    beside = collide([outer[i] * lattice_weights[i] for i in range(19)], outer[19] * (1.0 / LEVELS))
    beside.append(outer[19])
    shifted = list(beside)
    for k, i in enumerate(sideways):
        step = velocities[i][1]
        shifted[i] = jnp.where(lane % 4 == (2 if step == 1 else 1), wrapped[k], roll(beside[i], step, 1))
    for i in range(20):
        side[i] = shifted[i]
        post_side[i] = beside[i]
    row_lane = lanes((1, 128))
    for members, to, source, at_x in ((forward, after, ahead, AHEAD_ROW), (backward, before, behind, BEHIND_ROW)):
        extra = [jnp.zeros((1, 128), F32)] * 2
        for j, i in enumerate(members):
            extra[j // 4] = jnp.where(row_lane // 32 == j % 4, roll(shifted[i][at_x, :], 32 * (j % 4), 1), extra[j // 4])
            step = velocities[i][1]
            if step == 0:
                continue
            for z in range(1, 7):
                tile, at = row_place(j, z)
                lane_at, start = (0, 4 * z + 1) if step == 1 else (127, 4 * z + 2)
                fixed = roll(beside[i][at_x, :], lane_at - start, 1)
                chunks[to, 6 + tile, at, :] = jnp.where(row_lane == lane_at, fixed, source[tile, at, :])
        chunks[to, 9, 6:7, :] = extra[0]
        chunks[to, 9, 7:8, :] = extra[1]
    for group in range(2):
        for tile in range(3):
            held = [jnp.zeros((8, 128), F32)] * 2
            place, shift = (lane + 32 * group) % 128, 96 * group
            for _, _, slot, i, z in [n for n in NEAR if n[:2] == (group, tile)]:
                main = p1[i, z] if i < 19 else codes[z].astype(F32)
                step = velocities[i][1] if i < 19 else 0
                first = last = main
                if step == 1:
                    first = jnp.where(ends, roll(beside[i], 127 - 4 * z, 1), main)
                elif step == -1:
                    last = jnp.where(ends, roll(beside[i], 125 - 4 * z, 1), main)
                else:
                    first = jnp.where(lane == 127, roll(beside[i], 126 - 4 * z, 1), main)
                    last = jnp.where(lane == 0, roll(beside[i], -(4 * z + 2), 1), main)
                held[0] = jnp.where(place < 18 * slot, held[0], roll(first, 18 * slot + 1 + shift, 1))
                held[1] = jnp.where(place < 18 * slot, held[1], roll(last, 18 * slot - 111 + shift, 1))
            chunks[0, bases[group] + tile] = held[0]
            chunks[7, bases[group] + tile] = held[1]


def cross(outgoing, lane, shift_a, shift_b, frac_a, frac_b, outward=True):
    length = outgoing.shape[0]
    low = (lane // 32) % 2 == 1
    up_a, down_b = roll(outgoing, shift_a, 0), roll(outgoing, (length - shift_b) % length, 0)
    if outward:
        down_a, up_b = roll(outgoing, (length - shift_a) % length, 0), roll(outgoing, shift_b, 0)
        near = jnp.where(lane < 64, jnp.where(low, down_a, up_a), jnp.where(low, down_b, up_b))
    else:
        near = jnp.where(lane < 64, up_a, down_b)
    far = jnp.where(low, roll(near, -1, 0), roll(near, 1, 0))
    share = jnp.where(lane < 64, frac_a, frac_b)
    mixed = (1.0 - share) * near + share * far
    return jnp.where(low, roll(mixed, 32, 1), roll(mixed, -32, 1))


def spread_kernel(own, work):
    lane8 = lanes()
    upper, lower = set_bases()
    for item in range(20):
        tile, slot = divmod(item, 7)
        to = (64 - 18 * slot) % 128
        mine = (lane8 + to) % 128 >= 64
        for b in range(8):
            value = jnp.where(mine, own[b, upper + tile], own[b, lower + tile])
            work[item, 8 * b : 8 * b + 8, :] = roll(value, to, 1)


def plane_kernel(offsets_far, fractions_far, spread, near, far, ahead, behind, out, work, state, offsets, fractions, sems):
    copies = [
        pltpu.make_async_copy(offsets_far, offsets, sems.at[0]),
        pltpu.make_async_copy(fractions_far, fractions, sems.at[1]),
    ]
    for copy in copies:
        copy.start()
    length = work.shape[1]
    lane8 = lanes()
    lane = lanes((length, 128))
    here = lax.axis_index("gz")
    odd = here % 2
    after = (here + 1) % lax.axis_size("gz")
    me, peers = lax.axis_index("gx"), lax.axis_size("gx")
    for tile in range(4):
        out[(me + 1) % peers, 5 + tile] = ahead[tile]
        out[(me + peers - 1) % peers, 5 + tile] = behind[tile]

    def params(step):
        return (
            offsets[step, here],
            offsets[step, after],
            fractions[step, here].astype(F32) * (1.0 / FRAC_DEN),
            fractions[step, after].astype(F32) * (1.0 / FRAC_DEN),
        )

    for item in range(20):
        tile, slot = divmod(item, 7)
        to = (-18 * slot) % 128
        paired = (lane8 + to + 64 * (1 - odd)) % 128 < 64
        for b in range(8):
            at = slice(8 * b, 8 * b + 8)
            value = roll(jnp.where(paired, near[b, tile], far[b, tile]), to, 1)
            work[item, at, :] = jnp.where((lane8 >= 32) & (lane8 < 96), spread[item, at, :], value)
    for copy in copies:
        copy.wait()
    for j in range(5):
        step_x = velocities[rising[j]][0]
        state[sinking[j]] = roll(cross(work[j], lane, *params(0)), step_x, 0)
        state[rising[j]] = roll(work[14 + j], step_x, 0)
    for k, i in enumerate(level):
        state[i] = roll(work[5 + k], velocities[i][0], 0)
    for b in range(8):
        at = slice(8 * b, 8 * b + 8)
        post = collide([state[i, at, :] for i in range(19)], work[19, at, :] * (1.0 / LEVELS))
        for i in range(19):
            state[i, at, :] = roll(post[i], velocities[i][1], 1)
    final = []
    for i in level:
        final.append((i, None))
    for j in range(5):
        final.append((sinking[j], None))
    for j in range(5):
        final.append((rising[j], j))
    for n, (i, crossing) in enumerate(final):
        value = state[i]
        if crossing is not None:
            value = cross(value, lane, *params(1), outward=False)
        work[n] = roll(value, velocities[i][0], 0)
    part = lane8 // 16
    for b in range(8):
        for tile in range(5):
            packed = jnp.zeros((8, 128), F32)
            for k in range(4):
                n = tile * 4 + k
                if n >= 19:
                    break
                slot = 4 * (k // 2) + k % 2
                moved = roll(work[n, 8 * b : 8 * b + 8, :], 16 * slot - 33, 1)
                packed = jnp.where((part == slot) | (part == slot + 2), moved, packed)
            out[b, tile] = packed


def moved_x(value, i, z, rows_behind, rows_ahead, first_tile, row):
    if i in forward:
        tile, at = row_place(forward.index(i), z)
        source, to = rows_behind(first_tile + tile, at), 0
    elif i in backward:
        tile, at = row_place(backward.index(i), z)
        source, to = rows_ahead(first_tile + tile, at), 7
    else:
        return value
    return jnp.where(row == to, jnp.broadcast_to(source, (8, 128)), roll(value, velocities[i][0], 0))


def inner_kernel(p1, post_side, side, codes, own, p2, ahead, behind):
    lane, row = lanes(), rows()
    me, peers = lax.axis_index("gx"), lax.axis_size("gx")
    after, before = (me + 1) % peers, (me + peers - 1) % peers

    def rows_behind(tile, at):
        return own[before, tile, at, :]

    def rows_ahead(tile, at):
        return own[after, tile, at, :]

    f = []
    for i in range(19):
        value = side[i]
        for members, get, to in ((forward, rows_behind, 0), (backward, rows_ahead, 7)):
            if i in members:
                j = members.index(i)
                source = roll(get(9, slice(6 + j // 4, 7 + j // 4)), -32 * (j % 4), 1)
                value = jnp.where(row == to, jnp.broadcast_to(source, (8, 128)), roll(value, velocities[i][0], 0))
        f.append(roll(value, 4 * velocities[i][2], 1))
    beside = collide(f, side[19] * (1.0 / LEVELS))
    for j in range(2):
        ahead[3, 6 + j : 7 + j, :] = jnp.zeros((1, 128), F32)
        behind[3, 6 + j : 7 + j, :] = jnp.zeros((1, 128), F32)

    def mended(value, edge, step, z):
        if step == 1:
            return jnp.where(lane == 0, roll(edge, -(4 * z + 1), 1), value)
        if step == -1:
            return jnp.where(lane == 127, roll(edge, 127 - (4 * z + 2), 1), value)
        return value

    for z in range(1, 7):
        f = []
        for i in range(19):
            source = z - velocities[i][2]
            value = mended(p1[i, source], post_side[i], velocities[i][1], source)
            f.append(moved_x(value, i, z, rows_behind, rows_ahead, 6, row))
        post = collide(f, codes[z].astype(F32) * (1.0 / LEVELS))
        for i in range(19):
            step = velocities[i][1]
            value = mended(roll(post[i], step, 1), beside[i], step, z)
            p2[i, z - 1] = value
            if i in forward:
                tile, at = row_place(forward.index(i), z)
                ahead[tile, at, :] = value[AHEAD_ROW, :]
            if i in backward:
                tile, at = row_place(backward.index(i), z)
                behind[tile, at, :] = value[BEHIND_ROW, :]


def last_kernel(p2, planes, out, held_out, sems):
    lane, row = lanes(), rows()
    me, peers = lax.axis_index("gx"), lax.axis_size("gx")
    after, before = (me + 1) % peers, (me + peers - 1) % peers

    def rows_behind(tile, at):
        return planes[before, tile, at, :]

    def rows_ahead(tile, at):
        return planes[after, tile, at, :]

    target = []
    for group in range(2):
        z, inner = (7, 6) if group == 0 else (0, 1)
        inward = sinking if group == 0 else rising
        target.append([(i, z) for i in level] + [(i, inner) for i in inward] + [(i, z) for i in inward])
    part = lane // 16
    for tile in range(5):
        held = [planes[h, tile] for h in range(8)]
        for k in (1, 2, 4):
            fixed = part & k == 0
            for h in range(8):
                if h & k == 0:
                    lo, hi = held[h], held[h | k]
                    held[h] = jnp.where(fixed, lo, roll(hi, 16 * k, 1))
                    held[h | k] = jnp.where(fixed, roll(lo, -16 * k, 1), hi)
        for slot in range(8):
            n = tile * 4 + 2 * (slot // 4) + slot % 2
            if n < 19:
                i, z = target[0 if slot % 4 >= 2 else 1][n]
                held_out[i, z] = held[slot] * weight_inverse[i]
    copies = []
    for i in range(19):
        for z in range(8):
            source = z - velocities[i][2]
            if 1 <= source <= 6:
                value = moved_x(p2[i, source - 1], i, source, rows_behind, rows_ahead, 5, row)
                held_out[i, z] = value * weight_inverse[i]
        if i % 5 == 4 or i == 18:
            start = i - i % 5
            part = pl.ds(start, i + 1 - start)
            copies.append(pltpu.make_async_copy(held_out.at[part], out.at[part], sems.at[i // 5]))
            copies[-1].start()
    for copy in copies:
        copy.wait()


def run(kernel, outs, args, scratch=(), words=(), far_in=0, far_out=False, sems=0):
    near = pl.BlockSpec(memory_space=pltpu.VMEM)
    away = pl.BlockSpec(memory_space=pltpu.HBM)
    return pl.pallas_call(
        kernel,
        out_shape=[s if isinstance(s, jax.ShapeDtypeStruct) else jax.ShapeDtypeStruct(s, F32) for s in outs],
        in_specs=[away] * far_in + [near] * (len(args) - far_in),
        out_specs=[away if far_out else near] * len(outs),
        scratch_shapes=[pltpu.VMEM(s, F32) for s in scratch]
        + [pltpu.SMEM(s, jnp.int32) for s in words]
        + [pltpu.SemaphoreType.DMA((sems,))] * (sems > 0),
        compiler_params=pltpu.CompilerParams(vmem_limit_bytes=32 * 1024 * 1024),
    )(*args)


def swaps(to_near, to_far, axis):
    peers = lax.axis_size(axis)
    pair = [(i, i ^ 1) for i in range(peers)]
    other = [(i, (i + peers - 1) % peers if i % 2 == 0 else (i + 1) % peers) for i in range(peers)]
    far = lax.ppermute(to_far, axis, other)
    near = lax.ppermute(to_near, axis, pair)
    return near, far


def body(pops, codes, offsets, fractions):
    tile = (8, 128)
    pops, codes, offsets, fractions = (
        pltpu.with_memory_space_constraint(value, pltpu.HBM) for value in (pops, codes, offsets, fractions)
    )
    edges, pops, codes = run(
        edge_kernel,
        [(5,) + tile, (19, 8) + tile, jax.ShapeDtypeStruct((8,) + tile, jnp.int32)],
        (pops, codes),
        far_in=2,
        sems=6,
    )
    near, far = swaps(edges, edges, "gy")
    p1, wrapped, middle, ahead, behind = run(
        main_kernel,
        [(19, 8) + tile, (10,) + tile, (6, 6) + tile, (4,) + tile, (4,) + tile],
        (pops, codes),
    )
    chunks, post_side, side = run(
        edge_kernel_2,
        [(8, 10) + tile, (20,) + tile, (20,) + tile],
        (near, far, p1, codes, wrapped, middle, ahead, behind),
    )
    own = lax.all_to_all(chunks, "gx", 0, 0)
    near, far = swaps(own[:, 0:3], own[:, 3:6], "gz")
    p2, ahead, behind = run(
        inner_kernel,
        [(19, 6) + tile, (4,) + tile, (4,) + tile],
        (p1, post_side, side, codes, own),
    )
    (spread,) = run(spread_kernel, [(20, 64, 128)], (own,))
    (planes,) = run(
        plane_kernel,
        [(8, 9) + tile],
        (offsets, fractions, spread, near, far, ahead, behind),
        far_in=2,
        scratch=[(20, 64, 128), (19, 64, 128)],
        words=[offsets.shape] * 2,
        sems=2,
    )
    planes = lax.all_to_all(planes, "gx", 0, 0)
    (out,) = run(
        last_kernel, [(19, 8) + tile], (p2, planes), scratch=[(19, 8) + tile], far_out=True, sems=4
    )
    return out


def solution(mesh):
    in_specs = (P(None, "gz", "gx", "gy"), P("gz", "gx", "gy"), P(), P())
    out_specs = P(None, "gz", "gx", "gy")
    return jax.shard_map(body, mesh=mesh, in_specs=in_specs, out_specs=out_specs, check_vma=False)
```

```python
import jax
import jax.numpy as jnp
from jax import lax
from jax.experimental import pallas as pl
from jax.experimental.pallas import tpu as pltpu
from jax.sharding import PartitionSpec as P

LEVELS = 8
FRAC_DEN = 64
velocities = (
    (0, 0, 0), (1, 0, 0), (-1, 0, 0), (0, 1, 0), (0, -1, 0), (0, 0, 1), (0, 0, -1),
    (1, 1, 0), (-1, -1, 0), (1, -1, 0), (-1, 1, 0), (1, 0, 1), (-1, 0, -1), (1, 0, -1),
    (-1, 0, 1), (0, 1, 1), (0, -1, -1), (0, 1, -1), (0, -1, 1),
)
weight_inverse = (3.0,) + (18.0,) * 6 + (36.0,) * 12
lattice_weights = tuple(1.0 / v for v in weight_inverse)
relax_time = 0.9
pairs = ((1, 2), (3, 4), (5, 6), (7, 8), (9, 10), (11, 12), (13, 14), (15, 16), (17, 18))
rising = (5, 11, 14, 15, 18)
sinking = (6, 13, 12, 17, 16)
level = (0, 1, 2, 3, 4, 7, 8, 9, 10)
forward = (1, 7, 9, 11, 13)
backward = (2, 8, 10, 12, 14)
sideways = (3, 4, 7, 8, 9, 10, 15, 16, 17, 18)
F32 = jnp.float32


def roll(value, by, axis):
    if isinstance(by, int):
        by %= value.shape[axis]
        if by == 0:
            return value
    return pltpu.roll(value, by, axis)


def lanes(shape=(8, 128)):
    return lax.broadcasted_iota(jnp.int32, shape, 1)


def rows(shape=(8, 128)):
    return lax.broadcasted_iota(jnp.int32, shape, 0)


def collide(f, solid):
    density = f[0]
    for i, j in pairs:
        density = density + (f[i] + f[j])
    inverse = 1.0 / density
    speed = []
    for axis in range(3):
        total = None
        for i, j in pairs:
            moving = velocities[i][axis]
            if moving == 0:
                continue
            part = f[i] - f[j] if moving == 1 else f[j] - f[i]
            total = part if total is None else total + part
        speed.append(total * inverse)
    square = speed[0] * speed[0] + speed[1] * speed[1] + speed[2] * speed[2]
    fluid = 1.0 - solid
    keep = fluid * (1.0 - 1.0 / relax_time)
    pull = fluid * density * (1.0 / relax_time)
    calm = pull - 1.5 * square * pull
    post = [None] * 19
    post[0] = keep * f[0] + lattice_weights[0] * calm + solid * f[0]
    for i, j in pairs:
        along = None
        for axis in range(3):
            moving = velocities[i][axis]
            if moving == 0:
                continue
            if along is None:
                along = speed[axis] if moving == 1 else -speed[axis]
            else:
                along = along + speed[axis] if moving == 1 else along - speed[axis]
        weight = lattice_weights[i]
        flow = (3.0 * weight) * (pull * along)
        even = weight * calm + (1.5 * flow) * along
        post[i] = keep * f[i] + solid * f[j] + (even + flow)
        post[j] = keep * f[j] + solid * f[i] + (even - flow)
    return post


def edge_kernel(pops_far, codes_far, offsets_far, fractions_far, out, pops, codes, params, offsets, fractions, sems):
    lane = lanes()
    copies = (
        pltpu.make_async_copy(pops_far, pops, sems.at[0]),
        pltpu.make_async_copy(codes_far, codes, sems.at[1]),
        pltpu.make_async_copy(offsets_far, offsets, sems.at[2]),
        pltpu.make_async_copy(fractions_far, fractions, sems.at[3]),
    )
    for copy in copies:
        copy.start()
    for copy in copies:
        copy.wait()
    for tile in range(5):
        packed = jnp.zeros((8, 128), F32)
        for slot in range(4):
            item = tile * 4 + slot
            for z in range(8):
                start = slot * 32 + z * 4
                source = pops[item, z] if item < 19 else codes[z].astype(F32)
                moved = roll(source, start + 2, 1)
                packed = jnp.where(lane < start, packed, moved)
        out[tile] = packed
    here = lax.axis_index("gz")
    after = (here + 1) % lax.axis_size("gz")
    length = 8 * lax.axis_size("gx")
    row_lane = lanes((1, 128))
    low = (row_lane // 32) % 2 == 1
    for step in range(2):
        shift = jnp.where(row_lane < 64, offsets[step, here], offsets[step, after])
        shift = jnp.where(low, (length - shift) % length, shift)
        params[step : step + 1, :] = shift.astype(F32)
        share = jnp.where(row_lane < 64, fractions[step, here], fractions[step, after])
        params[step + 2 : step + 3, :] = share.astype(F32) * (1.0 / FRAC_DEN)


UPPER = [(i, 7) for i in rising] + [(i, 7) for i in level] + [(i, 6) for i in rising] + [(19, 7)]
LOWER = [(i, 0) for i in sinking] + [(i, 0) for i in level] + [(i, 1) for i in sinking] + [(19, 0)]
NEAR = [(group, tile, slot, i, z) for group, items in enumerate((UPPER, LOWER)) for tile in range(3) for slot, (i, z) in enumerate(items[7 * tile : 7 * tile + 7])]
still = tuple(i for i in range(19) if velocities[i][0] == 0)
ROWS = tuple(
    [(i, edge) for i in members] + [(i, inner) for i in members] + [(i, edge) for i in still] + [(19, edge)]
    for members, edge, inner in ((forward, 7, 6), (backward, 0, 1))
)


def set_bases():
    odd = lax.axis_index("gz") % 2
    return 3 * odd, 3 - 3 * odd


def put_rows(sides, i, z, value):
    target = z + (velocities[i][2] if i < 19 else 0)
    if 1 <= target <= 6:
        for side in range(2):
            for item, (member, x) in enumerate(ROWS[side]):
                if member == i:
                    sides[side, item, target : target + 1, :] = value[x : x + 1, :]


def main_kernel(pops, codes, p1, wrapped, chunks, sides):
    lane = lanes()
    side = [jnp.zeros((8, 128), F32) for _ in range(19)]
    for z in range(8):
        f = [pops[i, z] * lattice_weights[i] for i in range(19)]
        post = collide(f, codes[z].astype(F32) * (1.0 / LEVELS))
        for i in range(19):
            step = velocities[i][1]
            value = roll(post[i], step, 1)
            if step == 1:
                side[i] = jnp.where(lane == 4 * z + 2, roll(value, 4 * z + 2, 1), side[i])
            elif step == -1:
                side[i] = jnp.where(lane == 4 * z + 1, roll(value, 4 * z + 2, 1), side[i])
            p1[i, z] = value
            put_rows(sides, i, z, value)
        put_rows(sides, 19, z, codes[z].astype(F32))
    for k, i in enumerate(sideways):
        wrapped[k] = side[i]
    for group in range(2):
        for tile in range(3):
            held = [jnp.zeros((8, 128), F32)] * 6
            place = (lane + 32 * group) % 128
            for _, _, slot, i, z in [n for n in NEAR if n[:2] == (group, tile)]:
                source = p1[i, z] if i < 19 else codes[z].astype(F32)
                for d in range(1, 7):
                    moved = roll(source, 18 * slot - 16 * d + 1 + 96 * group, 1)
                    held[d - 1] = jnp.where(place < 18 * slot, held[d - 1], moved)
            for d in range(6):
                chunks[d, group * 3 + tile] = held[d]


def edge_kernel_2(near, far, p1, codes, wrapped, middle, sides, chunks, post_side, side, rows_near, rows_far):
    lane, row = lanes(), rows()
    ends = (lane == 0) | (lane == 127)
    bases = set_bases()
    for d in range(1, 7):
        for tile in range(3):
            chunks[d, bases[0] + tile] = middle[d - 1, tile]
            chunks[d, bases[1] + tile] = middle[d - 1, 3 + tile]
    outer = []
    paired = (lane // 2 + lax.axis_index("gy")) % 2 == 1
    for tile in range(5):
        both = jnp.where(paired, near[tile], far[tile])
        for slot in range(4):
            outer.append(roll(both, -32 * slot, 1))
    beside = collide([outer[i] * lattice_weights[i] for i in range(19)], outer[19] * (1.0 / LEVELS))
    beside.append(outer[19])
    shifted = list(beside)
    for k, i in enumerate(sideways):
        step = velocities[i][1]
        shifted[i] = jnp.where(lane % 4 == (2 if step == 1 else 1), wrapped[k], roll(beside[i], step, 1))
    for i in range(20):
        side[i] = shifted[i]
        post_side[i] = beside[i]
    even = lax.axis_index("gx") % 2 == 0
    for item in range(20):
        sent = []
        for k in range(2):
            i, x = ROWS[k][item]
            step_y, step_z = velocities[i][1:] if i < 19 else (0, 0)
            value = sides[k, item]
            if step_y:
                at, start = (0, 1) if step_y == 1 else (127, 2)
                spot = jnp.broadcast_to(beside[i][x : x + 1, :], (8, 128))
                spot = jnp.where(lane == 4 * (row - step_z) + start, spot, 0.0)
                value = jnp.where(lane == at, jnp.sum(spot, axis=1, keepdims=True), value)
            sent.append(jnp.where(row == 0, jnp.broadcast_to(shifted[i][x : x + 1, :], (8, 128)), value))
        rows_near[item] = jnp.where(even, sent[0], sent[1])
        rows_far[item] = jnp.where(even, sent[1], sent[0])
    for group in range(2):
        for tile in range(3):
            held = [jnp.zeros((8, 128), F32)] * 2
            place, shift = (lane + 32 * group) % 128, 96 * group
            for _, _, slot, i, z in [n for n in NEAR if n[:2] == (group, tile)]:
                main = p1[i, z] if i < 19 else codes[z].astype(F32)
                step = velocities[i][1] if i < 19 else 0
                first = last = main
                if step == 1:
                    first = jnp.where(ends, roll(beside[i], 127 - 4 * z, 1), main)
                elif step == -1:
                    last = jnp.where(ends, roll(beside[i], 125 - 4 * z, 1), main)
                else:
                    first = jnp.where(lane == 127, roll(beside[i], 126 - 4 * z, 1), main)
                    last = jnp.where(lane == 0, roll(beside[i], -(4 * z + 2), 1), main)
                held[0] = jnp.where(place < 18 * slot, held[0], roll(first, 18 * slot + 1 + shift, 1))
                held[1] = jnp.where(place < 18 * slot, held[1], roll(last, 18 * slot - 111 + shift, 1))
            chunks[0, bases[group] + tile] = held[0]
            chunks[7, bases[group] + tile] = held[1]


def cross(outgoing, lane, shift, share):
    length = outgoing.shape[0]
    low = (lane // 32) % 2 == 1
    near = outgoing
    bit = 1
    while bit < length:
        near = jnp.where((shift & bit) != 0, roll(near, bit, 0), near)
        bit *= 2
    far = jnp.where(low, roll(near, -1, 0), roll(near, 1, 0))
    mixed = (1.0 - share) * near + share * far
    return jnp.where(low, roll(mixed, 32, 1), roll(mixed, -32, 1))


def spread_kernel(own, work):
    lane8 = lanes()
    upper, lower = set_bases()
    for item in range(20):
        tile, slot = divmod(item, 7)
        to = (64 - 18 * slot) % 128
        mine = (lane8 + to) % 128 >= 64
        for b in range(8):
            value = jnp.where(mine, own[b, upper + tile], own[b, lower + tile])
            work[item, 8 * b : 8 * b + 8, :] = roll(value, to, 1)


def plane_kernel(params, spread, near, far, out, work, state):
    length = work.shape[1]
    lane8 = lanes()
    lane = lanes((length, 128))
    odd = lax.axis_index("gz") % 2

    def moves(step):
        return params[step : step + 1, :].astype(jnp.int32), params[step + 2 : step + 3, :]

    for item in range(20):
        tile, slot = divmod(item, 7)
        to = (-18 * slot) % 128
        paired = (lane8 + to + 64 * (1 - odd)) % 128 < 64
        for b in range(8):
            at = slice(8 * b, 8 * b + 8)
            value = roll(jnp.where(paired, near[b, tile], far[b, tile]), to, 1)
            work[item, at, :] = jnp.where((lane8 >= 32) & (lane8 < 96), spread[item, at, :], value)
    for j in range(5):
        step_x = velocities[rising[j]][0]
        state[sinking[j]] = roll(cross(work[j], lane, *moves(0)), step_x, 0)
        state[rising[j]] = roll(work[14 + j], step_x, 0)
    for k, i in enumerate(level):
        state[i] = roll(work[5 + k], velocities[i][0], 0)
    for b in range(8):
        at = slice(8 * b, 8 * b + 8)
        post = collide([state[i, at, :] for i in range(19)], work[19, at, :] * (1.0 / LEVELS))
        for i in range(19):
            state[i, at, :] = roll(post[i], velocities[i][1], 1)
    final = []
    for i in level:
        final.append((i, None))
    for j in range(5):
        final.append((sinking[j], None))
    for j in range(5):
        final.append((rising[j], j))
    for n, (i, crossing) in enumerate(final):
        value = state[i]
        if crossing is not None:
            value = cross(value, lane, *moves(1))
        work[n] = roll(value, velocities[i][0], 0)
    part = lane8 // 16
    for b in range(8):
        for tile in range(5):
            packed = jnp.zeros((8, 128), F32)
            for k in range(4):
                n = tile * 4 + k
                if n >= 19:
                    break
                slot = 4 * (k // 2) + k % 2
                moved = roll(work[n, 8 * b : 8 * b + 8, :], 16 * slot - 33, 1)
                packed = jnp.where((part == slot) | (part == slot + 2), moved, packed)
            out[b, tile] = packed


def moved_x(value, i, z, behind, ahead, row):
    if i in forward:
        source, to = behind(forward.index(i)), 0
    elif i in backward:
        source, to = ahead(backward.index(i)), 7
    else:
        return value
    return jnp.where(row == to, jnp.broadcast_to(source[z : z + 1, :], (8, 128)), roll(value, velocities[i][0], 0))


def inner_kernel(p1, post_side, side, codes, sent_near, sent_far, got_near, got_far, p2, ahead, behind):
    lane, row = lanes(), rows()
    even = lax.axis_index("gx") % 2 == 0
    own = (
        [jnp.where(even, sent_near[item], sent_far[item]) for item in range(5)],
        [jnp.where(even, sent_far[item], sent_near[item]) for item in range(5)],
    )
    got = (
        [jnp.where(even, got_far[item], got_near[item]) for item in range(20)],
        [jnp.where(even, got_near[item], got_far[item]) for item in range(20)],
    )

    def entering(k):
        f = [None] * 20
        for j, i in enumerate((forward, backward)[k]):
            f[i] = got[k][5 + j]
        for j, i in enumerate((backward, forward)[k]):
            f[i] = own[1 - k][j]
        for j, i in enumerate(still + (19,)):
            f[i] = got[k][10 + j]
        return f

    lines = [entering(k) for k in range(2)]
    f, corner = [], []
    for i in range(19):
        value = moved_x(side[i], i, 0, lambda j: got[0][j], lambda j: got[1][j], row)
        f.append(roll(value, 4 * velocities[i][2], 1))
        ends = [jnp.broadcast_to(lines[k][i][0:1, :], (8, 128)) for k in range(2)]
        corner.append(roll(jnp.where(row == 0, ends[0], ends[1]), 4 * velocities[i][2], 1))
    beside = collide(f, side[19] * (1.0 / LEVELS))
    ends = [jnp.broadcast_to(lines[k][19][0:1, :], (8, 128)) for k in range(2)]
    corner = collide(corner, jnp.where(row == 0, ends[0], ends[1]) * (1.0 / LEVELS))
    for k, (members, out) in enumerate(((forward, ahead), (backward, behind))):
        post = collide(lines[k][:19], lines[k][19] * (1.0 / LEVELS))
        for j, i in enumerate(members):
            step = velocities[i][1]
            value = roll(post[i], step, 1)
            if step:
                at, start = (0, 1) if step == 1 else (127, 2)
                spot = jnp.broadcast_to(corner[i][7 * k : 7 * k + 1, :], (8, 128))
                spot = jnp.where(lane == 4 * row + start, spot, 0.0)
                value = jnp.where(lane == at, jnp.sum(spot, axis=1, keepdims=True), value)
            out[j] = value

    def mended(value, edge, step, z):
        if step == 1:
            return jnp.where(lane == 0, roll(edge, -(4 * z + 1), 1), value)
        if step == -1:
            return jnp.where(lane == 127, roll(edge, 127 - (4 * z + 2), 1), value)
        return value

    for z in range(1, 7):
        f = []
        for i in range(19):
            source = z - velocities[i][2]
            value = mended(p1[i, source], post_side[i], velocities[i][1], source)
            f.append(moved_x(value, i, z, lambda j: got[0][j], lambda j: got[1][j], row))
        post = collide(f, codes[z].astype(F32) * (1.0 / LEVELS))
        for i in range(19):
            step = velocities[i][1]
            p2[i, z - 1] = mended(roll(post[i], step, 1), beside[i], step, z)


def last_kernel(p2, ahead, behind, planes, out, held_out, sems):
    lane, row = lanes(), rows()
    target = []
    for group in range(2):
        z, inner = (7, 6) if group == 0 else (0, 1)
        inward = sinking if group == 0 else rising
        target.append([(i, z) for i in level] + [(i, inner) for i in inward] + [(i, z) for i in inward])
    part = lane // 16
    for tile in range(5):
        held = [planes[h, tile] for h in range(8)]
        for k in (1, 2, 4):
            fixed = part & k == 0
            for h in range(8):
                if h & k == 0:
                    lo, hi = held[h], held[h | k]
                    held[h] = jnp.where(fixed, lo, roll(hi, 16 * k, 1))
                    held[h | k] = jnp.where(fixed, roll(lo, -16 * k, 1), hi)
        for slot in range(8):
            n = tile * 4 + 2 * (slot // 4) + slot % 2
            if n < 19:
                i, z = target[0 if slot % 4 >= 2 else 1][n]
                held_out[i, z] = held[slot] * weight_inverse[i]
    copies = []
    for i in range(19):
        for z in range(8):
            source = z - velocities[i][2]
            if 1 <= source <= 6:
                value = moved_x(p2[i, source - 1], i, source, lambda j: ahead[j], lambda j: behind[j], row)
                held_out[i, z] = value * weight_inverse[i]
        if i % 5 == 4 or i == 18:
            start = i - i % 5
            part = pl.ds(start, i + 1 - start)
            copies.append(pltpu.make_async_copy(held_out.at[part], out.at[part], sems.at[i // 5]))
            copies[-1].start()
    for copy in copies:
        copy.wait()


def run(kernel, outs, args, scratch=(), words=(), far_in=0, far_out=False, sems=0):
    near = pl.BlockSpec(memory_space=pltpu.VMEM)
    away = pl.BlockSpec(memory_space=pltpu.HBM)
    return pl.pallas_call(
        kernel,
        out_shape=[s if isinstance(s, jax.ShapeDtypeStruct) else jax.ShapeDtypeStruct(s, F32) for s in outs],
        in_specs=[away] * far_in + [near] * (len(args) - far_in),
        out_specs=[away if far_out else near] * len(outs),
        scratch_shapes=[pltpu.VMEM(s, F32) for s in scratch]
        + [pltpu.SMEM(s, jnp.int32) for s in words]
        + [pltpu.SemaphoreType.DMA((sems,))] * (sems > 0),
        compiler_params=pltpu.CompilerParams(vmem_limit_bytes=32 * 1024 * 1024),
    )(*args)


def swaps(to_near, to_far, axis):
    peers = lax.axis_size(axis)
    pair = [(i, i ^ 1) for i in range(peers)]
    other = [(i, (i + peers - 1) % peers if i % 2 == 0 else (i + 1) % peers) for i in range(peers)]
    far = lax.ppermute(to_far, axis, other)
    near = lax.ppermute(to_near, axis, pair)
    return near, far


def body(pops, codes, offsets, fractions):
    tile = (8, 128)
    pops, codes, offsets, fractions = (
        pltpu.with_memory_space_constraint(value, pltpu.HBM) for value in (pops, codes, offsets, fractions)
    )
    edges, pops, codes, params = run(
        edge_kernel,
        [(5,) + tile, (19, 8) + tile, jax.ShapeDtypeStruct((8,) + tile, jnp.int32), tile],
        (pops, codes, offsets, fractions),
        far_in=4,
        words=[offsets.shape] * 2,
        sems=4,
    )
    near, far = swaps(edges, edges, "gy")
    p1, wrapped, middle, sides = run(
        main_kernel,
        [(19, 8) + tile, (10,) + tile, (6, 6) + tile, (2, 20) + tile],
        (pops, codes),
    )
    chunks, post_side, side, sent_near, sent_far = run(
        edge_kernel_2,
        [(8, 6) + tile, (20,) + tile, (20,) + tile, (20,) + tile, (20,) + tile],
        (near, far, p1, codes, wrapped, middle, sides),
    )
    got_near, got_far = swaps(sent_near, sent_far, "gx")
    own = lax.all_to_all(chunks, "gx", 0, 0)
    near, far = swaps(own[:, 0:3], own[:, 3:6], "gz")
    (spread,) = run(spread_kernel, [(20, 64, 128)], (own,))
    p2, ahead, behind = run(
        inner_kernel,
        [(19, 6) + tile, (5,) + tile, (5,) + tile],
        (p1, post_side, side, codes, sent_near, sent_far, got_near, got_far),
    )
    (planes,) = run(
        plane_kernel,
        [(8, 5) + tile],
        (params, spread, near, far),
        scratch=[(20, 64, 128), (19, 64, 128)],
    )
    planes = lax.all_to_all(planes, "gx", 0, 0)
    (out,) = run(
        last_kernel, [(19, 8) + tile], (p2, ahead, behind, planes), scratch=[(19, 8) + tile], far_out=True, sems=4
    )
    return out


def solution(mesh):
    in_specs = (P(None, "gz", "gx", "gy"), P("gz", "gx", "gy"), P(), P())
    out_specs = P(None, "gz", "gx", "gy")
    return jax.shard_map(body, mesh=mesh, in_specs=in_specs, out_specs=out_specs, check_vma=False)
```

```python
import jax
import jax.numpy as jnp
from jax import lax
from jax.experimental import pallas as pl
from jax.experimental.pallas import tpu as pltpu
from jax.sharding import PartitionSpec as P

LEVELS = 8
FRAC_DEN = 64
velocities = (
    (0, 0, 0), (1, 0, 0), (-1, 0, 0), (0, 1, 0), (0, -1, 0), (0, 0, 1), (0, 0, -1),
    (1, 1, 0), (-1, -1, 0), (1, -1, 0), (-1, 1, 0), (1, 0, 1), (-1, 0, -1), (1, 0, -1),
    (-1, 0, 1), (0, 1, 1), (0, -1, -1), (0, 1, -1), (0, -1, 1),
)
weight_inverse = (3.0,) + (18.0,) * 6 + (36.0,) * 12
lattice_weights = tuple(1.0 / v for v in weight_inverse)
relax_time = 0.9
pairs = ((1, 2), (3, 4), (5, 6), (7, 8), (9, 10), (11, 12), (13, 14), (15, 16), (17, 18))
rising = (5, 11, 14, 15, 18)
sinking = (6, 13, 12, 17, 16)
level = (0, 1, 2, 3, 4, 7, 8, 9, 10)
forward = (1, 7, 9, 11, 13)
backward = (2, 8, 10, 12, 14)
sideways = (3, 4, 7, 8, 9, 10, 15, 16, 17, 18)
F32 = jnp.float32


def roll(value, by, axis):
    if isinstance(by, int):
        by %= value.shape[axis]
        if by == 0:
            return value
    return pltpu.roll(value, by, axis)


def lanes(shape=(8, 128)):
    return lax.broadcasted_iota(jnp.int32, shape, 1)


def rows(shape=(8, 128)):
    return lax.broadcasted_iota(jnp.int32, shape, 0)


def collide(f, solid):
    density = f[0]
    for i, j in pairs:
        density = density + (f[i] + f[j])
    inverse = 1.0 / density
    speed = []
    for axis in range(3):
        total = None
        for i, j in pairs:
            moving = velocities[i][axis]
            if moving == 0:
                continue
            part = f[i] - f[j] if moving == 1 else f[j] - f[i]
            total = part if total is None else total + part
        speed.append(total * inverse)
    square = speed[0] * speed[0] + speed[1] * speed[1] + speed[2] * speed[2]
    fluid = 1.0 - solid
    keep = fluid * (1.0 - 1.0 / relax_time)
    pull = fluid * density * (1.0 / relax_time)
    calm = pull - 1.5 * square * pull
    post = [None] * 19
    post[0] = keep * f[0] + lattice_weights[0] * calm + solid * f[0]
    for i, j in pairs:
        along = None
        for axis in range(3):
            moving = velocities[i][axis]
            if moving == 0:
                continue
            if along is None:
                along = speed[axis] if moving == 1 else -speed[axis]
            else:
                along = along + speed[axis] if moving == 1 else along - speed[axis]
        weight = lattice_weights[i]
        flow = (3.0 * weight) * (pull * along)
        even = weight * calm + (1.5 * flow) * along
        post[i] = keep * f[i] + solid * f[j] + (even + flow)
        post[j] = keep * f[j] + solid * f[i] + (even - flow)
    return post


def edge_kernel(pops_far, codes_far, offsets_far, fractions_far, out, pops, codes, params, offsets, fractions, sems):
    lane = lanes()
    copies = (
        pltpu.make_async_copy(pops_far, pops, sems.at[0]),
        pltpu.make_async_copy(codes_far, codes, sems.at[1]),
        pltpu.make_async_copy(offsets_far, offsets, sems.at[2]),
        pltpu.make_async_copy(fractions_far, fractions, sems.at[3]),
    )
    for copy in copies:
        copy.start()
    for copy in copies:
        copy.wait()
    for tile in range(5):
        packed = jnp.zeros((8, 128), F32)
        for slot in range(4):
            item = tile * 4 + slot
            for z in range(8):
                start = slot * 32 + z * 4
                source = pops[item, z] if item < 19 else codes[z].astype(F32)
                moved = roll(source, start + 2, 1)
                packed = jnp.where(lane < start, packed, moved)
        out[tile] = packed
    here = lax.axis_index("gz")
    after = (here + 1) % lax.axis_size("gz")
    length = 8 * lax.axis_size("gx")
    row_lane = lanes((1, 128))
    low = (row_lane // 32) % 2 == 1
    for step in range(2):
        shift = jnp.where(row_lane < 64, offsets[step, here], offsets[step, after])
        shift = jnp.where(low, (length - shift) % length, shift)
        params[step : step + 1, :] = shift.astype(F32)
        share = jnp.where(row_lane < 64, fractions[step, here], fractions[step, after])
        params[step + 2 : step + 3, :] = share.astype(F32) * (1.0 / FRAC_DEN)


UPPER = [(i, 7) for i in rising] + [(i, 7) for i in level] + [(i, 6) for i in rising] + [(19, 7)]
LOWER = [(i, 0) for i in sinking] + [(i, 0) for i in level] + [(i, 1) for i in sinking] + [(19, 0)]
NEAR = [(group, tile, slot, i, z) for group, items in enumerate((UPPER, LOWER)) for tile in range(3) for slot, (i, z) in enumerate(items[7 * tile : 7 * tile + 7])]
still = tuple(i for i in range(19) if velocities[i][0] == 0)
ROWS = tuple(
    [(i, edge) for i in members] + [(i, inner) for i in members] + [(i, edge) for i in still] + [(19, edge)]
    for members, edge, inner in ((forward, 7, 6), (backward, 0, 1))
)


def set_bases():
    odd = lax.axis_index("gz") % 2
    return 3 * odd, 3 - 3 * odd


def put_rows(sides, i, z, value):
    target = z + (velocities[i][2] if i < 19 else 0)
    if 1 <= target <= 6:
        for side in range(2):
            for item, (member, x) in enumerate(ROWS[side]):
                if member == i:
                    sides[side, item, target : target + 1, :] = value[x : x + 1, :]


def main_kernel(pops, codes, p1, wrapped, chunks, sides):
    lane = lanes()
    side = [jnp.zeros((8, 128), F32) for _ in range(19)]
    for z in range(8):
        f = [pops[i, z] * lattice_weights[i] for i in range(19)]
        post = collide(f, codes[z].astype(F32) * (1.0 / LEVELS))
        for i in range(19):
            step = velocities[i][1]
            value = roll(post[i], step, 1)
            if step == 1:
                side[i] = jnp.where(lane == 4 * z + 2, roll(value, 4 * z + 2, 1), side[i])
            elif step == -1:
                side[i] = jnp.where(lane == 4 * z + 1, roll(value, 4 * z + 2, 1), side[i])
            p1[i, z] = value
            put_rows(sides, i, z, value)
        put_rows(sides, 19, z, codes[z].astype(F32))
    for k, i in enumerate(sideways):
        wrapped[k] = side[i]
    for group in range(2):
        for tile in range(3):
            held = [jnp.zeros((8, 128), F32)] * 6
            place = (lane + 32 * group) % 128
            for _, _, slot, i, z in [n for n in NEAR if n[:2] == (group, tile)]:
                source = p1[i, z] if i < 19 else codes[z].astype(F32)
                for d in range(1, 7):
                    moved = roll(source, 18 * slot - 16 * d + 1 + 96 * group, 1)
                    held[d - 1] = jnp.where(place < 18 * slot, held[d - 1], moved)
            for d in range(6):
                chunks[d, group * 3 + tile] = held[d]


def edge_kernel_2(near, far, p1, codes, wrapped, middle, sides, chunks, post_side, side, rows_ahead, rows_behind):
    lane, row = lanes(), rows()
    ends = (lane == 0) | (lane == 127)
    bases = set_bases()
    for d in range(1, 7):
        for tile in range(3):
            chunks[d, bases[0] + tile] = middle[d - 1, tile]
            chunks[d, bases[1] + tile] = middle[d - 1, 3 + tile]
    outer = []
    paired = (lane // 2 + lax.axis_index("gy")) % 2 == 1
    for tile in range(5):
        both = jnp.where(paired, near[tile], far[tile])
        for slot in range(4):
            outer.append(roll(both, -32 * slot, 1))
    beside = collide([outer[i] * lattice_weights[i] for i in range(19)], outer[19] * (1.0 / LEVELS))
    beside.append(outer[19])
    shifted = list(beside)
    for k, i in enumerate(sideways):
        step = velocities[i][1]
        shifted[i] = jnp.where(lane % 4 == (2 if step == 1 else 1), wrapped[k], roll(beside[i], step, 1))
    for i in range(20):
        side[i] = shifted[i]
        post_side[i] = beside[i]
    for item in range(20):
        sent = []
        for k in range(2):
            i, x = ROWS[k][item]
            step_y, step_z = velocities[i][1:] if i < 19 else (0, 0)
            value = sides[k, item]
            if step_y:
                at, start = (0, 1) if step_y == 1 else (127, 2)
                spot = jnp.broadcast_to(beside[i][x : x + 1, :], (8, 128))
                spot = jnp.where(lane == 4 * (row - step_z) + start, spot, 0.0)
                value = jnp.where(lane == at, jnp.sum(spot, axis=1, keepdims=True), value)
            sent.append(jnp.where(row == 0, jnp.broadcast_to(shifted[i][x : x + 1, :], (8, 128)), value))
        rows_ahead[item], rows_behind[item] = sent
    for group in range(2):
        for tile in range(3):
            held = [jnp.zeros((8, 128), F32)] * 2
            place, shift = (lane + 32 * group) % 128, 96 * group
            for _, _, slot, i, z in [n for n in NEAR if n[:2] == (group, tile)]:
                main = p1[i, z] if i < 19 else codes[z].astype(F32)
                step = velocities[i][1] if i < 19 else 0
                first = last = main
                if step == 1:
                    first = jnp.where(ends, roll(beside[i], 127 - 4 * z, 1), main)
                elif step == -1:
                    last = jnp.where(ends, roll(beside[i], 125 - 4 * z, 1), main)
                else:
                    first = jnp.where(lane == 127, roll(beside[i], 126 - 4 * z, 1), main)
                    last = jnp.where(lane == 0, roll(beside[i], -(4 * z + 2), 1), main)
                held[0] = jnp.where(place < 18 * slot, held[0], roll(first, 18 * slot + 1 + shift, 1))
                held[1] = jnp.where(place < 18 * slot, held[1], roll(last, 18 * slot - 111 + shift, 1))
            chunks[0, bases[group] + tile] = held[0]
            chunks[7, bases[group] + tile] = held[1]


def cross(outgoing, lane, shift, share):
    length = outgoing.shape[0]
    low = (lane // 32) % 2 == 1
    near = outgoing
    bit = 1
    while bit < length:
        near = jnp.where((shift & bit) != 0, roll(near, bit, 0), near)
        bit *= 2
    far = jnp.where(low, roll(near, -1, 0), roll(near, 1, 0))
    mixed = (1.0 - share) * near + share * far
    return jnp.where(low, roll(mixed, 32, 1), roll(mixed, -32, 1))


def spread_kernel(own, work):
    lane8 = lanes()
    upper, lower = set_bases()
    for item in range(20):
        tile, slot = divmod(item, 7)
        to = (64 - 18 * slot) % 128
        mine = (lane8 + to) % 128 >= 64
        for b in range(8):
            value = jnp.where(mine, own[b, upper + tile], own[b, lower + tile])
            work[item, 8 * b : 8 * b + 8, :] = roll(value, to, 1)


def plane_kernel(params, spread, near, far, out, work, state):
    length = work.shape[1]
    lane8 = lanes()
    lane = lanes((length, 128))
    odd = lax.axis_index("gz") % 2

    def moves(step):
        return params[step : step + 1, :].astype(jnp.int32), params[step + 2 : step + 3, :]

    for item in range(20):
        tile, slot = divmod(item, 7)
        to = (-18 * slot) % 128
        paired = (lane8 + to + 64 * (1 - odd)) % 128 < 64
        for b in range(8):
            at = slice(8 * b, 8 * b + 8)
            value = roll(jnp.where(paired, near[b, tile], far[b, tile]), to, 1)
            work[item, at, :] = jnp.where((lane8 >= 32) & (lane8 < 96), spread[item, at, :], value)
    for j in range(5):
        step_x = velocities[rising[j]][0]
        state[sinking[j]] = roll(cross(work[j], lane, *moves(0)), step_x, 0)
        state[rising[j]] = roll(work[14 + j], step_x, 0)
    for k, i in enumerate(level):
        state[i] = roll(work[5 + k], velocities[i][0], 0)
    for b in range(8):
        at = slice(8 * b, 8 * b + 8)
        post = collide([state[i, at, :] for i in range(19)], work[19, at, :] * (1.0 / LEVELS))
        for i in range(19):
            state[i, at, :] = roll(post[i], velocities[i][1], 1)
    final = []
    for i in level:
        final.append((i, None))
    for j in range(5):
        final.append((sinking[j], None))
    for j in range(5):
        final.append((rising[j], j))
    for n, (i, crossing) in enumerate(final):
        value = state[i]
        if crossing is not None:
            value = cross(value, lane, *moves(1))
        work[n] = roll(value, velocities[i][0], 0)
    part = lane8 // 16
    for b in range(8):
        for tile in range(5):
            packed = jnp.zeros((8, 128), F32)
            for k in range(4):
                n = tile * 4 + k
                if n >= 19:
                    break
                slot = 4 * (k // 2) + k % 2
                moved = roll(work[n, 8 * b : 8 * b + 8, :], 16 * slot - 33, 1)
                packed = jnp.where((part == slot) | (part == slot + 2), moved, packed)
            out[b, tile] = packed


def moved_x(value, i, z, behind, ahead, row):
    if i in forward:
        source, to = behind(forward.index(i)), 0
    elif i in backward:
        source, to = ahead(backward.index(i)), 7
    else:
        return value
    return jnp.where(row == to, jnp.broadcast_to(source[z : z + 1, :], (8, 128)), roll(value, velocities[i][0], 0))


def inner_kernel(p1, post_side, side, codes, sent_ahead, sent_behind, from_behind, from_ahead, p2, ahead, behind):
    lane, row = lanes(), rows()
    own, got = (sent_ahead, sent_behind), (from_behind, from_ahead)

    def entering(k):
        f = [None] * 20
        for j, i in enumerate((forward, backward)[k]):
            f[i] = got[k][5 + j]
        for j, i in enumerate((backward, forward)[k]):
            f[i] = own[1 - k][j]
        for j, i in enumerate(still + (19,)):
            f[i] = got[k][10 + j]
        return f

    lines = [entering(k) for k in range(2)]
    f, corner = [], []
    for i in range(19):
        value = moved_x(side[i], i, 0, lambda j: got[0][j], lambda j: got[1][j], row)
        f.append(roll(value, 4 * velocities[i][2], 1))
        ends = [jnp.broadcast_to(lines[k][i][0:1, :], (8, 128)) for k in range(2)]
        corner.append(roll(jnp.where(row == 0, ends[0], ends[1]), 4 * velocities[i][2], 1))
    beside = collide(f, side[19] * (1.0 / LEVELS))
    ends = [jnp.broadcast_to(lines[k][19][0:1, :], (8, 128)) for k in range(2)]
    corner = collide(corner, jnp.where(row == 0, ends[0], ends[1]) * (1.0 / LEVELS))
    for k, (members, out) in enumerate(((forward, ahead), (backward, behind))):
        post = collide(lines[k][:19], lines[k][19] * (1.0 / LEVELS))
        for j, i in enumerate(members):
            step = velocities[i][1]
            value = roll(post[i], step, 1)
            if step:
                at, start = (0, 1) if step == 1 else (127, 2)
                spot = jnp.broadcast_to(corner[i][7 * k : 7 * k + 1, :], (8, 128))
                spot = jnp.where(lane == 4 * row + start, spot, 0.0)
                value = jnp.where(lane == at, jnp.sum(spot, axis=1, keepdims=True), value)
            out[j] = value

    def mended(value, edge, step, z):
        if step == 1:
            return jnp.where(lane == 0, roll(edge, -(4 * z + 1), 1), value)
        if step == -1:
            return jnp.where(lane == 127, roll(edge, 127 - (4 * z + 2), 1), value)
        return value

    for z in range(1, 7):
        f = []
        for i in range(19):
            source = z - velocities[i][2]
            value = mended(p1[i, source], post_side[i], velocities[i][1], source)
            f.append(moved_x(value, i, z, lambda j: got[0][j], lambda j: got[1][j], row))
        post = collide(f, codes[z].astype(F32) * (1.0 / LEVELS))
        for i in range(19):
            step = velocities[i][1]
            p2[i, z - 1] = mended(roll(post[i], step, 1), beside[i], step, z)


def last_kernel(p2, ahead, behind, planes, out, held_out, sems):
    lane, row = lanes(), rows()
    target = []
    for group in range(2):
        z, inner = (7, 6) if group == 0 else (0, 1)
        inward = sinking if group == 0 else rising
        target.append([(i, z) for i in level] + [(i, inner) for i in inward] + [(i, z) for i in inward])
    part = lane // 16
    for tile in range(5):
        held = [planes[h, tile] for h in range(8)]
        for k in (1, 2, 4):
            fixed = part & k == 0
            for h in range(8):
                if h & k == 0:
                    lo, hi = held[h], held[h | k]
                    held[h] = jnp.where(fixed, lo, roll(hi, 16 * k, 1))
                    held[h | k] = jnp.where(fixed, roll(lo, -16 * k, 1), hi)
        for slot in range(8):
            n = tile * 4 + 2 * (slot // 4) + slot % 2
            if n < 19:
                i, z = target[0 if slot % 4 >= 2 else 1][n]
                held_out[i, z] = held[slot] * weight_inverse[i]
    copies = []
    for i in range(19):
        for z in range(8):
            source = z - velocities[i][2]
            if 1 <= source <= 6:
                value = moved_x(p2[i, source - 1], i, source, lambda j: ahead[j], lambda j: behind[j], row)
                held_out[i, z] = value * weight_inverse[i]
        if i % 5 == 4 or i == 18:
            start = i - i % 5
            part = pl.ds(start, i + 1 - start)
            copies.append(pltpu.make_async_copy(held_out.at[part], out.at[part], sems.at[i // 5]))
            copies[-1].start()
    for copy in copies:
        copy.wait()


def run(kernel, outs, args, scratch=(), words=(), far_in=0, far_out=False, sems=0):
    near = pl.BlockSpec(memory_space=pltpu.VMEM)
    away = pl.BlockSpec(memory_space=pltpu.HBM)
    return pl.pallas_call(
        kernel,
        out_shape=[s if isinstance(s, jax.ShapeDtypeStruct) else jax.ShapeDtypeStruct(s, F32) for s in outs],
        in_specs=[away] * far_in + [near] * (len(args) - far_in),
        out_specs=[away if far_out else near] * len(outs),
        scratch_shapes=[pltpu.VMEM(s, F32) for s in scratch]
        + [pltpu.SMEM(s, jnp.int32) for s in words]
        + [pltpu.SemaphoreType.DMA((sems,))] * (sems > 0),
        compiler_params=pltpu.CompilerParams(vmem_limit_bytes=32 * 1024 * 1024),
    )(*args)


def neighbours(value_up, value_down, axis):
    peers = lax.axis_size(axis)
    up = [(i, (i + 1) % peers) for i in range(peers)]
    down = [(j, i) for i, j in up]
    return lax.ppermute(value_up, axis, up), lax.ppermute(value_down, axis, down)


def swaps(to_near, to_far, axis):
    peers = lax.axis_size(axis)
    pair = [(i, i ^ 1) for i in range(peers)]
    other = [(i, (i + peers - 1) % peers if i % 2 == 0 else (i + 1) % peers) for i in range(peers)]
    far = lax.ppermute(to_far, axis, other)
    near = lax.ppermute(to_near, axis, pair)
    return near, far


def body(pops, codes, offsets, fractions):
    tile = (8, 128)
    pops, codes, offsets, fractions = (
        pltpu.with_memory_space_constraint(value, pltpu.HBM) for value in (pops, codes, offsets, fractions)
    )
    edges, pops, codes, params = run(
        edge_kernel,
        [(5,) + tile, (19, 8) + tile, jax.ShapeDtypeStruct((8,) + tile, jnp.int32), tile],
        (pops, codes, offsets, fractions),
        far_in=4,
        words=[offsets.shape] * 2,
        sems=4,
    )
    near, far = swaps(edges, edges, "gy")
    p1, wrapped, middle, sides = run(
        main_kernel,
        [(19, 8) + tile, (10,) + tile, (6, 6) + tile, (2, 20) + tile],
        (pops, codes),
    )
    chunks, post_side, side, sent_ahead, sent_behind = run(
        edge_kernel_2,
        [(8, 6) + tile, (20,) + tile, (20,) + tile, (20,) + tile, (20,) + tile],
        (near, far, p1, codes, wrapped, middle, sides),
    )
    from_behind, from_ahead = neighbours(sent_ahead, sent_behind, "gx")
    own = lax.all_to_all(chunks, "gx", 0, 0)
    near, far = swaps(own[:, 0:3], own[:, 3:6], "gz")
    (spread,) = run(spread_kernel, [(20, 64, 128)], (own,))
    p2, ahead, behind = run(
        inner_kernel,
        [(19, 6) + tile, (5,) + tile, (5,) + tile],
        (p1, post_side, side, codes, sent_ahead, sent_behind, from_behind, from_ahead),
    )
    (planes,) = run(
        plane_kernel,
        [(8, 5) + tile],
        (params, spread, near, far),
        scratch=[(20, 64, 128), (19, 64, 128)],
    )
    planes = lax.all_to_all(planes, "gx", 0, 0)
    (out,) = run(
        last_kernel, [(19, 8) + tile], (p2, ahead, behind, planes), scratch=[(19, 8) + tile], far_out=True, sems=4
    )
    return out


def solution(mesh):
    in_specs = (P(None, "gz", "gx", "gy"), P("gz", "gx", "gy"), P(), P())
    out_specs = P(None, "gz", "gx", "gy")
    return jax.shard_map(body, mesh=mesh, in_specs=in_specs, out_specs=out_specs, check_vma=False)
```

```python
import jax
import jax.numpy as jnp
from jax import lax
from jax.experimental import pallas as pl
from jax.experimental.pallas import tpu as pltpu
from jax.sharding import PartitionSpec as P

LEVELS = 8
FRAC_DEN = 64
velocities = (
    (0, 0, 0), (1, 0, 0), (-1, 0, 0), (0, 1, 0), (0, -1, 0), (0, 0, 1), (0, 0, -1),
    (1, 1, 0), (-1, -1, 0), (1, -1, 0), (-1, 1, 0), (1, 0, 1), (-1, 0, -1), (1, 0, -1),
    (-1, 0, 1), (0, 1, 1), (0, -1, -1), (0, 1, -1), (0, -1, 1),
)
weight_inverse = (3.0,) + (18.0,) * 6 + (36.0,) * 12
lattice_weights = tuple(1.0 / v for v in weight_inverse)
relax_time = 0.9
pairs = ((1, 2), (3, 4), (5, 6), (7, 8), (9, 10), (11, 12), (13, 14), (15, 16), (17, 18))
rising = (5, 11, 14, 15, 18)
sinking = (6, 13, 12, 17, 16)
level = (0, 1, 2, 3, 4, 7, 8, 9, 10)
forward = (1, 7, 9, 11, 13)
backward = (2, 8, 10, 12, 14)
sideways = (3, 4, 7, 8, 9, 10, 15, 16, 17, 18)
F32 = jnp.float32


def roll(value, by, axis):
    if isinstance(by, int):
        by %= value.shape[axis]
        if by == 0:
            return value
    return pltpu.roll(value, by, axis)


def lanes(shape=(8, 128)):
    return lax.broadcasted_iota(jnp.int32, shape, 1)


def rows(shape=(8, 128)):
    return lax.broadcasted_iota(jnp.int32, shape, 0)


def collide(f, solid):
    density = f[0]
    for i, j in pairs:
        density = density + (f[i] + f[j])
    inverse = 1.0 / density
    speed = []
    for axis in range(3):
        total = None
        for i, j in pairs:
            moving = velocities[i][axis]
            if moving == 0:
                continue
            part = f[i] - f[j] if moving == 1 else f[j] - f[i]
            total = part if total is None else total + part
        speed.append(total * inverse)
    square = speed[0] * speed[0] + speed[1] * speed[1] + speed[2] * speed[2]
    fluid = 1.0 - solid
    keep = fluid * (1.0 - 1.0 / relax_time)
    pull = fluid * density * (1.0 / relax_time)
    calm = pull - 1.5 * square * pull
    post = [None] * 19
    post[0] = keep * f[0] + lattice_weights[0] * calm + solid * f[0]
    for i, j in pairs:
        along = None
        for axis in range(3):
            moving = velocities[i][axis]
            if moving == 0:
                continue
            if along is None:
                along = speed[axis] if moving == 1 else -speed[axis]
            else:
                along = along + speed[axis] if moving == 1 else along - speed[axis]
        weight = lattice_weights[i]
        flow = (3.0 * weight) * (pull * along)
        even = weight * calm + (1.5 * flow) * along
        post[i] = keep * f[i] + solid * f[j] + (even + flow)
        post[j] = keep * f[j] + solid * f[i] + (even - flow)
    return post


def edge_kernel(pops_far, codes_far, offsets_far, fractions_far, out, pops, codes, params, offsets, fractions, sems):
    lane = lanes()
    copies = (
        pltpu.make_async_copy(pops_far, pops, sems.at[0]),
        pltpu.make_async_copy(codes_far, codes, sems.at[1]),
        pltpu.make_async_copy(offsets_far, offsets, sems.at[2]),
        pltpu.make_async_copy(fractions_far, fractions, sems.at[3]),
    )
    for copy in copies:
        copy.start()
    for copy in copies:
        copy.wait()
    for tile in range(5):
        packed = jnp.zeros((8, 128), F32)
        for slot in range(4):
            item = tile * 4 + slot
            for z in range(8):
                start = slot * 32 + z * 4
                source = pops[item, z] if item < 19 else codes[z].astype(F32)
                moved = roll(source, start + 2, 1)
                packed = jnp.where(lane < start, packed, moved)
        out[tile] = packed
    here = lax.axis_index("gz")
    after = (here + 1) % lax.axis_size("gz")
    length = 8 * lax.axis_size("gx")
    row_lane = lanes((1, 128))
    low = (row_lane // 32) % 2 == 1
    for step in range(2):
        shift = jnp.where(row_lane < 64, offsets[step, here], offsets[step, after])
        shift = jnp.where(low, (length - shift) % length, shift)
        params[step : step + 1, :] = shift.astype(F32)
        share = jnp.where(row_lane < 64, fractions[step, here], fractions[step, after])
        params[step + 2 : step + 3, :] = share.astype(F32) * (1.0 / FRAC_DEN)


UPPER = [(i, 7) for i in rising] + [(i, 7) for i in level] + [(i, 6) for i in rising] + [(19, 7)]
LOWER = [(i, 0) for i in sinking] + [(i, 0) for i in level] + [(i, 1) for i in sinking] + [(19, 0)]
NEAR = [(group, tile, slot, i, z) for group, items in enumerate((UPPER, LOWER)) for tile in range(3) for slot, (i, z) in enumerate(items[7 * tile : 7 * tile + 7])]
still = tuple(i for i in range(19) if velocities[i][0] == 0)
ROWS = tuple(
    [(i, edge) for i in members] + [(i, inner) for i in members] + [(i, edge) for i in still] + [(19, edge)]
    for members, edge, inner in ((forward, 7, 6), (backward, 0, 1))
)


def set_bases():
    odd = lax.axis_index("gz") % 2
    return 3 * odd, 3 - 3 * odd


def put_rows(sides, i, z, value):
    target = z + (velocities[i][2] if i < 19 else 0)
    if 1 <= target <= 6:
        for side in range(2):
            for item, (member, x) in enumerate(ROWS[side]):
                if member == i:
                    sides[side, item, target : target + 1, :] = value[x : x + 1, :]


def main_kernel(pops, codes, p1, wrapped, chunks, sides):
    lane = lanes()
    side = [jnp.zeros((8, 128), F32) for _ in range(19)]
    for z in range(8):
        f = [pops[i, z] * lattice_weights[i] for i in range(19)]
        post = collide(f, codes[z].astype(F32) * (1.0 / LEVELS))
        for i in range(19):
            step = velocities[i][1]
            value = roll(post[i], step, 1)
            if step == 1:
                side[i] = jnp.where(lane == 4 * z + 2, roll(value, 4 * z + 2, 1), side[i])
            elif step == -1:
                side[i] = jnp.where(lane == 4 * z + 1, roll(value, 4 * z + 2, 1), side[i])
            p1[i, z] = value
            put_rows(sides, i, z, value)
        put_rows(sides, 19, z, codes[z].astype(F32))
    for k, i in enumerate(sideways):
        wrapped[k] = side[i]
    for group in range(2):
        for tile in range(3):
            held = [jnp.zeros((8, 128), F32)] * 6
            place = (lane + 32 * group) % 128
            for _, _, slot, i, z in [n for n in NEAR if n[:2] == (group, tile)]:
                source = p1[i, z] if i < 19 else codes[z].astype(F32)
                for d in range(1, 7):
                    moved = roll(source, 18 * slot - 16 * d + 1 + 96 * group, 1)
                    held[d - 1] = jnp.where(place < 18 * slot, held[d - 1], moved)
            for d in range(6):
                chunks[d, group * 3 + tile] = held[d]


def edge_kernel_2(far, near, p1, codes, wrapped, middle, sides, chunks, post_side, side, rows_ahead, rows_behind):
    lane, row = lanes(), rows()
    ends = (lane == 0) | (lane == 127)
    bases = set_bases()
    for d in range(1, 7):
        for tile in range(3):
            chunks[d, bases[0] + tile] = middle[d - 1, tile]
            chunks[d, bases[1] + tile] = middle[d - 1, 3 + tile]
    outer = []
    paired = (lane // 2 + lax.axis_index("gy")) % 2 == 1
    for tile in range(5):
        both = jnp.where(paired, near[tile], far[tile])
        for slot in range(4):
            outer.append(roll(both, -32 * slot, 1))
    beside = collide([outer[i] * lattice_weights[i] for i in range(19)], outer[19] * (1.0 / LEVELS))
    beside.append(outer[19])
    shifted = list(beside)
    for k, i in enumerate(sideways):
        step = velocities[i][1]
        shifted[i] = jnp.where(lane % 4 == (2 if step == 1 else 1), wrapped[k], roll(beside[i], step, 1))
    for i in range(20):
        side[i] = shifted[i]
        post_side[i] = beside[i]
    for item in range(20):
        sent = []
        for k in range(2):
            i, x = ROWS[k][item]
            step_y, step_z = velocities[i][1:] if i < 19 else (0, 0)
            value = sides[k, item]
            if step_y:
                at, start = (0, 1) if step_y == 1 else (127, 2)
                spot = jnp.broadcast_to(beside[i][x : x + 1, :], (8, 128))
                spot = jnp.where(lane == 4 * (row - step_z) + start, spot, 0.0)
                value = jnp.where(lane == at, jnp.sum(spot, axis=1, keepdims=True), value)
            sent.append(jnp.where(row == 0, jnp.broadcast_to(shifted[i][x : x + 1, :], (8, 128)), value))
        rows_ahead[item], rows_behind[item] = sent
    for group in range(2):
        for tile in range(3):
            held = [jnp.zeros((8, 128), F32)] * 2
            place, shift = (lane + 32 * group) % 128, 96 * group
            for _, _, slot, i, z in [n for n in NEAR if n[:2] == (group, tile)]:
                main = p1[i, z] if i < 19 else codes[z].astype(F32)
                step = velocities[i][1] if i < 19 else 0
                first = last = main
                if step == 1:
                    first = jnp.where(ends, roll(beside[i], 127 - 4 * z, 1), main)
                elif step == -1:
                    last = jnp.where(ends, roll(beside[i], 125 - 4 * z, 1), main)
                else:
                    first = jnp.where(lane == 127, roll(beside[i], 126 - 4 * z, 1), main)
                    last = jnp.where(lane == 0, roll(beside[i], -(4 * z + 2), 1), main)
                held[0] = jnp.where(place < 18 * slot, held[0], roll(first, 18 * slot + 1 + shift, 1))
                held[1] = jnp.where(place < 18 * slot, held[1], roll(last, 18 * slot - 111 + shift, 1))
            chunks[0, bases[group] + tile] = held[0]
            chunks[7, bases[group] + tile] = held[1]


def cross(outgoing, lane, shift, share):
    length = outgoing.shape[0]
    low = (lane // 32) % 2 == 1
    near = outgoing
    bit = 1
    while bit < length:
        near = jnp.where((shift & bit) != 0, roll(near, bit, 0), near)
        bit *= 2
    far = jnp.where(low, roll(near, -1, 0), roll(near, 1, 0))
    mixed = (1.0 - share) * near + share * far
    return jnp.where(low, roll(mixed, 32, 1), roll(mixed, -32, 1))


def spread_kernel(own, work):
    lane8 = lanes()
    upper, lower = set_bases()
    for item in range(20):
        tile, slot = divmod(item, 7)
        to = (64 - 18 * slot) % 128
        mine = (lane8 + to) % 128 >= 64
        for b in range(8):
            value = jnp.where(mine, own[b, upper + tile], own[b, lower + tile])
            work[item, 8 * b : 8 * b + 8, :] = roll(value, to, 1)


def plane_kernel(params, spread, far, near, out, work, state):
    length = work.shape[1]
    lane8 = lanes()
    lane = lanes((length, 128))
    odd = lax.axis_index("gz") % 2

    def moves(step):
        return params[step : step + 1, :].astype(jnp.int32), params[step + 2 : step + 3, :]

    for item in range(20):
        tile, slot = divmod(item, 7)
        to = (-18 * slot) % 128
        paired = (lane8 + to + 64 * (1 - odd)) % 128 < 64
        for b in range(8):
            at = slice(8 * b, 8 * b + 8)
            value = roll(jnp.where(paired, near[b, tile], far[b, tile]), to, 1)
            work[item, at, :] = jnp.where((lane8 >= 32) & (lane8 < 96), spread[item, at, :], value)
    for j in range(5):
        step_x = velocities[rising[j]][0]
        state[sinking[j]] = roll(cross(work[j], lane, *moves(0)), step_x, 0)
        state[rising[j]] = roll(work[14 + j], step_x, 0)
    for k, i in enumerate(level):
        state[i] = roll(work[5 + k], velocities[i][0], 0)
    for b in range(8):
        at = slice(8 * b, 8 * b + 8)
        post = collide([state[i, at, :] for i in range(19)], work[19, at, :] * (1.0 / LEVELS))
        for i in range(19):
            state[i, at, :] = roll(post[i], velocities[i][1], 1)
    final = []
    for i in level:
        final.append((i, None))
    for j in range(5):
        final.append((sinking[j], None))
    for j in range(5):
        final.append((rising[j], j))
    for n, (i, crossing) in enumerate(final):
        value = state[i]
        if crossing is not None:
            value = cross(value, lane, *moves(1))
        work[n] = roll(value, velocities[i][0], 0)
    part = lane8 // 16
    for b in range(8):
        for tile in range(5):
            packed = jnp.zeros((8, 128), F32)
            for k in range(4):
                n = tile * 4 + k
                if n >= 19:
                    break
                slot = 4 * (k // 2) + k % 2
                moved = roll(work[n, 8 * b : 8 * b + 8, :], 16 * slot - 33, 1)
                packed = jnp.where((part == slot) | (part == slot + 2), moved, packed)
            out[b, tile] = packed


def moved_x(value, i, z, behind, ahead, row):
    if i in forward:
        source, to = behind(forward.index(i)), 0
    elif i in backward:
        source, to = ahead(backward.index(i)), 7
    else:
        return value
    return jnp.where(row == to, jnp.broadcast_to(source[z : z + 1, :], (8, 128)), roll(value, velocities[i][0], 0))


def mended(value, edge, step, z):
    lane = lanes()
    if step == 1:
        return jnp.where(lane == 0, roll(edge, -(4 * z + 1), 1), value)
    if step == -1:
        return jnp.where(lane == 127, roll(edge, 127 - (4 * z + 2), 1), value)
    return value


def arrive_kernel(p1, post_side, arrived):
    for z in range(1, 7):
        for i in range(19):
            source = z - velocities[i][2]
            value = mended(p1[i, source], post_side[i], velocities[i][1], source)
            arrived[i, z - 1] = roll(value, velocities[i][0], 0)


def inner_kernel(arrived, side, codes, sent_ahead, sent_behind, from_behind, from_ahead, p2, ahead, behind):
    lane, row = lanes(), rows()
    own, got = (sent_ahead, sent_behind), (from_behind, from_ahead)

    def entering(k):
        f = [None] * 20
        for j, i in enumerate((forward, backward)[k]):
            f[i] = got[k][5 + j]
        for j, i in enumerate((backward, forward)[k]):
            f[i] = own[1 - k][j]
        for j, i in enumerate(still + (19,)):
            f[i] = got[k][10 + j]
        return f

    lines = [entering(k) for k in range(2)]
    f, corner = [], []
    for i in range(19):
        value = moved_x(side[i], i, 0, lambda j: got[0][j], lambda j: got[1][j], row)
        f.append(roll(value, 4 * velocities[i][2], 1))
        ends = [jnp.broadcast_to(lines[k][i][0:1, :], (8, 128)) for k in range(2)]
        corner.append(roll(jnp.where(row == 0, ends[0], ends[1]), 4 * velocities[i][2], 1))
    beside = collide(f, side[19] * (1.0 / LEVELS))
    ends = [jnp.broadcast_to(lines[k][19][0:1, :], (8, 128)) for k in range(2)]
    corner = collide(corner, jnp.where(row == 0, ends[0], ends[1]) * (1.0 / LEVELS))
    for k, (members, out) in enumerate(((forward, ahead), (backward, behind))):
        post = collide(lines[k][:19], lines[k][19] * (1.0 / LEVELS))
        for j, i in enumerate(members):
            step = velocities[i][1]
            value = roll(post[i], step, 1)
            if step:
                at, start = (0, 1) if step == 1 else (127, 2)
                spot = jnp.broadcast_to(corner[i][7 * k : 7 * k + 1, :], (8, 128))
                spot = jnp.where(lane == 4 * row + start, spot, 0.0)
                value = jnp.where(lane == at, jnp.sum(spot, axis=1, keepdims=True), value)
            out[j] = value

    for z in range(1, 7):
        f = []
        for i in range(19):
            value = arrived[i, z - 1]
            for members, k, at in ((forward, 0, 0), (backward, 1, 7)):
                if i in members:
                    entered = got[k][members.index(i)][z : z + 1, :]
                    value = jnp.where(row == at, jnp.broadcast_to(entered, (8, 128)), value)
            f.append(value)
        post = collide(f, codes[z].astype(F32) * (1.0 / LEVELS))
        for i in range(19):
            step = velocities[i][1]
            p2[i, z - 1] = mended(roll(post[i], step, 1), beside[i], step, z)


def last_kernel(p2, ahead, behind, planes, out, held_out, sems):
    lane, row = lanes(), rows()
    target = []
    for group in range(2):
        z, inner = (7, 6) if group == 0 else (0, 1)
        inward = sinking if group == 0 else rising
        target.append([(i, z) for i in level] + [(i, inner) for i in inward] + [(i, z) for i in inward])
    part = lane // 16
    for tile in range(5):
        held = [planes[h, tile] for h in range(8)]
        for k in (1, 2, 4):
            fixed = part & k == 0
            for h in range(8):
                if h & k == 0:
                    lo, hi = held[h], held[h | k]
                    held[h] = jnp.where(fixed, lo, roll(hi, 16 * k, 1))
                    held[h | k] = jnp.where(fixed, roll(lo, -16 * k, 1), hi)
        for slot in range(8):
            n = tile * 4 + 2 * (slot // 4) + slot % 2
            if n < 19:
                i, z = target[0 if slot % 4 >= 2 else 1][n]
                held_out[i, z] = held[slot] * weight_inverse[i]
    copies = []
    for i in range(19):
        for z in range(8):
            source = z - velocities[i][2]
            if 1 <= source <= 6:
                value = moved_x(p2[i, source - 1], i, source, lambda j: ahead[j], lambda j: behind[j], row)
                held_out[i, z] = value * weight_inverse[i]
        if i % 5 == 4 or i == 18:
            start = i - i % 5
            part = pl.ds(start, i + 1 - start)
            copies.append(pltpu.make_async_copy(held_out.at[part], out.at[part], sems.at[i // 5]))
            copies[-1].start()
    for copy in copies:
        copy.wait()


def run(kernel, outs, args, scratch=(), words=(), far_in=0, far_out=False, sems=0):
    near = pl.BlockSpec(memory_space=pltpu.VMEM)
    away = pl.BlockSpec(memory_space=pltpu.HBM)
    return pl.pallas_call(
        kernel,
        out_shape=[s if isinstance(s, jax.ShapeDtypeStruct) else jax.ShapeDtypeStruct(s, F32) for s in outs],
        in_specs=[away] * far_in + [near] * (len(args) - far_in),
        out_specs=[away if far_out else near] * len(outs),
        scratch_shapes=[pltpu.VMEM(s, F32) for s in scratch]
        + [pltpu.SMEM(s, jnp.int32) for s in words]
        + [pltpu.SemaphoreType.DMA((sems,))] * (sems > 0),
        compiler_params=pltpu.CompilerParams(vmem_limit_bytes=32 * 1024 * 1024),
    )(*args)


def neighbours(value_up, value_down, axis):
    peers = lax.axis_size(axis)
    up = [(i, (i + 1) % peers) for i in range(peers)]
    down = [(j, i) for i, j in up]
    return lax.ppermute(value_up, axis, up), lax.ppermute(value_down, axis, down)


def swaps(to_near, to_far, axis):
    peers = lax.axis_size(axis)
    pair = [(i, i ^ 1) for i in range(peers)]
    other = [(i, (i + peers - 1) % peers if i % 2 == 0 else (i + 1) % peers) for i in range(peers)]
    far = lax.ppermute(to_far, axis, other)
    near = lax.ppermute(to_near, axis, pair)
    return near, far


def body(pops, codes, offsets, fractions):
    tile = (8, 128)
    pops, codes, offsets, fractions = (
        pltpu.with_memory_space_constraint(value, pltpu.HBM) for value in (pops, codes, offsets, fractions)
    )
    edges, pops, codes, params = run(
        edge_kernel,
        [(5,) + tile, (19, 8) + tile, jax.ShapeDtypeStruct((8,) + tile, jnp.int32), tile],
        (pops, codes, offsets, fractions),
        far_in=4,
        words=[offsets.shape] * 2,
        sems=4,
    )
    near, far = swaps(edges, edges, "gy")
    p1, wrapped, middle, sides = run(
        main_kernel,
        [(19, 8) + tile, (10,) + tile, (6, 6) + tile, (2, 20) + tile],
        (pops, codes),
    )
    chunks, post_side, side, sent_ahead, sent_behind = run(
        edge_kernel_2,
        [(8, 6) + tile, (20,) + tile, (20,) + tile, (20,) + tile, (20,) + tile],
        (far, near, p1, codes, wrapped, middle, sides),
    )
    from_behind, from_ahead = neighbours(sent_ahead, sent_behind, "gx")
    own = lax.all_to_all(chunks, "gx", 0, 0)
    near, far = swaps(own[:, 0:3], own[:, 3:6], "gz")
    (spread,) = run(spread_kernel, [(20, 64, 128)], (own,))
    (arrived,) = run(arrive_kernel, [(19, 6) + tile], (p1, post_side))
    p2, ahead, behind = run(
        inner_kernel,
        [(19, 6) + tile, (5,) + tile, (5,) + tile],
        (arrived, side, codes, sent_ahead, sent_behind, from_behind, from_ahead),
    )
    (planes,) = run(
        plane_kernel,
        [(8, 5) + tile],
        (params, spread, far, near),
        scratch=[(20, 64, 128), (19, 64, 128)],
    )
    planes = lax.all_to_all(planes, "gx", 0, 0)
    (out,) = run(
        last_kernel, [(19, 8) + tile], (p2, ahead, behind, planes), scratch=[(19, 8) + tile], far_out=True, sems=4
    )
    return out


def solution(mesh):
    in_specs = (P(None, "gz", "gx", "gy"), P("gz", "gx", "gy"), P(), P())
    out_specs = P(None, "gz", "gx", "gy")
    return jax.shard_map(body, mesh=mesh, in_specs=in_specs, out_specs=out_specs, check_vma=False)
```

```python
import jax
import jax.numpy as jnp
from jax import lax
from jax.experimental import pallas as pl
from jax.experimental.pallas import tpu as pltpu
from jax.sharding import PartitionSpec as P

LEVELS = 8
FRAC_DEN = 64
velocities = (
    (0, 0, 0), (1, 0, 0), (-1, 0, 0), (0, 1, 0), (0, -1, 0), (0, 0, 1), (0, 0, -1),
    (1, 1, 0), (-1, -1, 0), (1, -1, 0), (-1, 1, 0), (1, 0, 1), (-1, 0, -1), (1, 0, -1),
    (-1, 0, 1), (0, 1, 1), (0, -1, -1), (0, 1, -1), (0, -1, 1),
)
weight_inverse = (3.0,) + (18.0,) * 6 + (36.0,) * 12
lattice_weights = tuple(1.0 / v for v in weight_inverse)
relax_time = 0.9
pairs = ((1, 2), (3, 4), (5, 6), (7, 8), (9, 10), (11, 12), (13, 14), (15, 16), (17, 18))
rising = (5, 11, 14, 15, 18)
sinking = (6, 13, 12, 17, 16)
level = (0, 1, 2, 3, 4, 7, 8, 9, 10)
forward = (1, 7, 9, 11, 13)
backward = (2, 8, 10, 12, 14)
sideways = (3, 4, 7, 8, 9, 10, 15, 16, 17, 18)
F32 = jnp.float32


def roll(value, by, axis):
    if isinstance(by, int):
        by %= value.shape[axis]
        if by == 0:
            return value
    return pltpu.roll(value, by, axis)


def lanes(shape=(8, 128)):
    return lax.broadcasted_iota(jnp.int32, shape, 1)


def rows(shape=(8, 128)):
    return lax.broadcasted_iota(jnp.int32, shape, 0)


def collide(f, solid):
    density = f[0]
    for i, j in pairs:
        density = density + (f[i] + f[j])
    inverse = 1.0 / density
    speed = []
    for axis in range(3):
        total = None
        for i, j in pairs:
            moving = velocities[i][axis]
            if moving == 0:
                continue
            part = f[i] - f[j] if moving == 1 else f[j] - f[i]
            total = part if total is None else total + part
        speed.append(total * inverse)
    square = speed[0] * speed[0] + speed[1] * speed[1] + speed[2] * speed[2]
    fluid = 1.0 - solid
    keep = fluid * (1.0 - 1.0 / relax_time)
    pull = fluid * density * (1.0 / relax_time)
    calm = pull - 1.5 * square * pull
    post = [None] * 19
    post[0] = keep * f[0] + lattice_weights[0] * calm + solid * f[0]
    for i, j in pairs:
        along = None
        for axis in range(3):
            moving = velocities[i][axis]
            if moving == 0:
                continue
            if along is None:
                along = speed[axis] if moving == 1 else -speed[axis]
            else:
                along = along + speed[axis] if moving == 1 else along - speed[axis]
        weight = lattice_weights[i]
        flow = (3.0 * weight) * (pull * along)
        even = weight * calm + (1.5 * flow) * along
        post[i] = keep * f[i] + solid * f[j] + (even + flow)
        post[j] = keep * f[j] + solid * f[i] + (even - flow)
    return post


def edge_kernel(pops_far, codes_far, out, pops, codes, sems):
    lane = lanes()
    copies = (
        pltpu.make_async_copy(pops_far, pops, sems.at[0]),
        pltpu.make_async_copy(codes_far, codes, sems.at[1]),
    )
    for copy in copies:
        copy.start()
    for copy in copies:
        copy.wait()
    for tile in range(5):
        packed = jnp.zeros((8, 128), F32)
        for slot in range(4):
            item = tile * 4 + slot
            for z in range(8):
                start = slot * 32 + z * 4
                source = pops[item, z] if item < 19 else codes[z].astype(F32)
                moved = roll(source, start + 2, 1)
                packed = jnp.where(lane < start, packed, moved)
        out[tile] = packed


UPPER = [(i, 7) for i in rising] + [(i, 7) for i in level] + [(i, 6) for i in rising] + [(19, 7)]
LOWER = [(i, 0) for i in sinking] + [(i, 0) for i in level] + [(i, 1) for i in sinking] + [(19, 0)]
NEAR = [(group, tile, slot, i, z) for group, items in enumerate((UPPER, LOWER)) for tile in range(3) for slot, (i, z) in enumerate(items[7 * tile : 7 * tile + 7])]
still = tuple(i for i in range(19) if velocities[i][0] == 0)
ROWS = tuple(
    [(i, edge) for i in members] + [(i, inner) for i in members] + [(i, edge) for i in still] + [(19, edge)]
    for members, edge, inner in ((forward, 7, 6), (backward, 0, 1))
)


def set_bases():
    odd = lax.axis_index("gz") % 2
    return 3 * odd, 3 - 3 * odd


def put_rows(sides, i, z, value):
    target = z + (velocities[i][2] if i < 19 else 0)
    if 1 <= target <= 6:
        for side in range(2):
            for item, (member, x) in enumerate(ROWS[side]):
                if member == i:
                    sides[side, item, target : target + 1, :] = value[x : x + 1, :]


def main_kernel(offsets_far, fractions_far, pops, codes, p1, wrapped, chunks, sides, params, offsets, fractions, sems):
    lane = lanes()
    copies = (
        pltpu.make_async_copy(offsets_far, offsets, sems.at[0]),
        pltpu.make_async_copy(fractions_far, fractions, sems.at[1]),
    )
    for copy in copies:
        copy.start()
    side = [jnp.zeros((8, 128), F32) for _ in range(19)]
    for z in range(8):
        f = [pops[i, z] * lattice_weights[i] for i in range(19)]
        post = collide(f, codes[z].astype(F32) * (1.0 / LEVELS))
        for i in range(19):
            step = velocities[i][1]
            value = roll(post[i], step, 1)
            if step == 1:
                side[i] = jnp.where(lane == 4 * z + 2, roll(value, 4 * z + 2, 1), side[i])
            elif step == -1:
                side[i] = jnp.where(lane == 4 * z + 1, roll(value, 4 * z + 2, 1), side[i])
            p1[i, z] = value
            put_rows(sides, i, z, value)
        put_rows(sides, 19, z, codes[z].astype(F32))
    for k, i in enumerate(sideways):
        wrapped[k] = side[i]
    for group in range(2):
        for tile in range(3):
            held = [jnp.zeros((8, 128), F32)] * 6
            place = (lane + 32 * group) % 128
            for _, _, slot, i, z in [n for n in NEAR if n[:2] == (group, tile)]:
                source = p1[i, z] if i < 19 else codes[z].astype(F32)
                for d in range(1, 7):
                    moved = roll(source, 18 * slot - 16 * d + 1 + 96 * group, 1)
                    held[d - 1] = jnp.where(place < 18 * slot, held[d - 1], moved)
            for d in range(6):
                chunks[d, group * 3 + tile] = held[d]
    for copy in copies:
        copy.wait()
    here = lax.axis_index("gz")
    after = (here + 1) % lax.axis_size("gz")
    length = 8 * lax.axis_size("gx")
    row_lane = lanes((1, 128))
    low = (row_lane // 32) % 2 == 1
    for step in range(2):
        shift = jnp.where(row_lane < 64, offsets[step, here], offsets[step, after])
        shift = jnp.where(low, (length - shift) % length, shift)
        params[step : step + 1, :] = shift.astype(F32)
        share = jnp.where(row_lane < 64, fractions[step, here], fractions[step, after])
        params[step + 2 : step + 3, :] = share.astype(F32) * (1.0 / FRAC_DEN)


def edge_kernel_2(far, near, p1, codes, wrapped, middle, sides, chunks, post_side, side, rows_ahead, rows_behind):
    lane, row = lanes(), rows()
    ends = (lane == 0) | (lane == 127)
    bases = set_bases()
    for d in range(1, 7):
        for tile in range(3):
            chunks[d, bases[0] + tile] = middle[d - 1, tile]
            chunks[d, bases[1] + tile] = middle[d - 1, 3 + tile]
    outer = []
    paired = (lane // 2 + lax.axis_index("gy")) % 2 == 1
    for tile in range(5):
        both = jnp.where(paired, near[tile], far[tile])
        for slot in range(4):
            outer.append(roll(both, -32 * slot, 1))
    beside = collide([outer[i] * lattice_weights[i] for i in range(19)], outer[19] * (1.0 / LEVELS))
    beside.append(outer[19])
    shifted = list(beside)
    for k, i in enumerate(sideways):
        step = velocities[i][1]
        shifted[i] = jnp.where(lane % 4 == (2 if step == 1 else 1), wrapped[k], roll(beside[i], step, 1))
    for i in range(20):
        side[i] = shifted[i]
        post_side[i] = beside[i]
    for item in range(20):
        sent = []
        for k in range(2):
            i, x = ROWS[k][item]
            step_y, step_z = velocities[i][1:] if i < 19 else (0, 0)
            value = sides[k, item]
            if step_y:
                at, start = (0, 1) if step_y == 1 else (127, 2)
                spot = jnp.broadcast_to(beside[i][x : x + 1, :], (8, 128))
                spot = jnp.where(lane == 4 * (row - step_z) + start, spot, 0.0)
                value = jnp.where(lane == at, jnp.sum(spot, axis=1, keepdims=True), value)
            sent.append(jnp.where(row == 0, jnp.broadcast_to(shifted[i][x : x + 1, :], (8, 128)), value))
        rows_ahead[item], rows_behind[item] = sent
    for group in range(2):
        for tile in range(3):
            held = [jnp.zeros((8, 128), F32)] * 2
            place, shift = (lane + 32 * group) % 128, 96 * group
            for _, _, slot, i, z in [n for n in NEAR if n[:2] == (group, tile)]:
                main = p1[i, z] if i < 19 else codes[z].astype(F32)
                step = velocities[i][1] if i < 19 else 0
                first = last = main
                if step == 1:
                    first = jnp.where(ends, roll(beside[i], 127 - 4 * z, 1), main)
                elif step == -1:
                    last = jnp.where(ends, roll(beside[i], 125 - 4 * z, 1), main)
                else:
                    first = jnp.where(lane == 127, roll(beside[i], 126 - 4 * z, 1), main)
                    last = jnp.where(lane == 0, roll(beside[i], -(4 * z + 2), 1), main)
                held[0] = jnp.where(place < 18 * slot, held[0], roll(first, 18 * slot + 1 + shift, 1))
                held[1] = jnp.where(place < 18 * slot, held[1], roll(last, 18 * slot - 111 + shift, 1))
            chunks[0, bases[group] + tile] = held[0]
            chunks[7, bases[group] + tile] = held[1]


def cross(outgoing, lane, shift, share):
    length = outgoing.shape[0]
    low = (lane // 32) % 2 == 1
    near = outgoing
    bit = 1
    while bit < length:
        near = jnp.where((shift & bit) != 0, roll(near, bit, 0), near)
        bit *= 2
    far = jnp.where(low, roll(near, -1, 0), roll(near, 1, 0))
    mixed = (1.0 - share) * near + share * far
    return jnp.where(low, roll(mixed, 32, 1), roll(mixed, -32, 1))


def spread_kernel(own, work):
    lane8 = lanes()
    upper, lower = set_bases()
    for item in range(20):
        tile, slot = divmod(item, 7)
        to = (64 - 18 * slot) % 128
        mine = (lane8 + to) % 128 >= 64
        for b in range(8):
            value = jnp.where(mine, own[b, upper + tile], own[b, lower + tile])
            work[item, 8 * b : 8 * b + 8, :] = roll(value, to, 1)


def plane_kernel(params, spread, far, near, out, work, state):
    length = work.shape[1]
    lane8 = lanes()
    lane = lanes((length, 128))
    odd = lax.axis_index("gz") % 2

    def moves(step):
        return params[step : step + 1, :].astype(jnp.int32), params[step + 2 : step + 3, :]

    for item in range(20):
        tile, slot = divmod(item, 7)
        to = (-18 * slot) % 128
        paired = (lane8 + to + 64 * (1 - odd)) % 128 < 64
        for b in range(8):
            at = slice(8 * b, 8 * b + 8)
            value = roll(jnp.where(paired, near[b, tile], far[b, tile]), to, 1)
            work[item, at, :] = jnp.where((lane8 >= 32) & (lane8 < 96), spread[item, at, :], value)
    for j in range(5):
        step_x = velocities[rising[j]][0]
        state[sinking[j]] = roll(cross(work[j], lane, *moves(0)), step_x, 0)
        state[rising[j]] = roll(work[14 + j], step_x, 0)
    for k, i in enumerate(level):
        state[i] = roll(work[5 + k], velocities[i][0], 0)
    for b in range(8):
        at = slice(8 * b, 8 * b + 8)
        post = collide([state[i, at, :] for i in range(19)], work[19, at, :] * (1.0 / LEVELS))
        for i in range(19):
            state[i, at, :] = roll(post[i], velocities[i][1], 1)
    final = []
    for i in level:
        final.append((i, None))
    for j in range(5):
        final.append((sinking[j], None))
    for j in range(5):
        final.append((rising[j], j))
    for n, (i, crossing) in enumerate(final):
        value = state[i]
        if crossing is not None:
            value = cross(value, lane, *moves(1))
        work[n] = roll(value, velocities[i][0], 0)
    part = lane8 // 16
    for b in range(8):
        for tile in range(5):
            packed = jnp.zeros((8, 128), F32)
            for k in range(4):
                n = tile * 4 + k
                if n >= 19:
                    break
                slot = 4 * (k // 2) + k % 2
                moved = roll(work[n, 8 * b : 8 * b + 8, :], 16 * slot - 33, 1)
                packed = jnp.where((part == slot) | (part == slot + 2), moved, packed)
            out[b, tile] = packed


def moved_x(value, i, z, behind, ahead, row):
    if i in forward:
        source, to = behind(forward.index(i)), 0
    elif i in backward:
        source, to = ahead(backward.index(i)), 7
    else:
        return value
    return jnp.where(row == to, jnp.broadcast_to(source[z : z + 1, :], (8, 128)), roll(value, velocities[i][0], 0))


def mended(value, edge, step, z):
    lane = lanes()
    if step == 1:
        return jnp.where(lane == 0, roll(edge, -(4 * z + 1), 1), value)
    if step == -1:
        return jnp.where(lane == 127, roll(edge, 127 - (4 * z + 2), 1), value)
    return value


def arrive_kernel(p1, post_side, arrived):
    for z in range(1, 7):
        for i in range(19):
            source = z - velocities[i][2]
            value = mended(p1[i, source], post_side[i], velocities[i][1], source)
            arrived[i, z - 1] = roll(value, velocities[i][0], 0)


def inner_kernel(arrived, side, codes, sent_ahead, sent_behind, from_behind, from_ahead, p2, ahead, behind):
    lane, row = lanes(), rows()
    own, got = (sent_ahead, sent_behind), (from_behind, from_ahead)

    def entering(k):
        f = [None] * 20
        for j, i in enumerate((forward, backward)[k]):
            f[i] = got[k][5 + j]
        for j, i in enumerate((backward, forward)[k]):
            f[i] = own[1 - k][j]
        for j, i in enumerate(still + (19,)):
            f[i] = got[k][10 + j]
        return f

    lines = [entering(k) for k in range(2)]
    f, corner = [], []
    for i in range(19):
        value = moved_x(side[i], i, 0, lambda j: got[0][j], lambda j: got[1][j], row)
        f.append(roll(value, 4 * velocities[i][2], 1))
        ends = [jnp.broadcast_to(lines[k][i][0:1, :], (8, 128)) for k in range(2)]
        corner.append(roll(jnp.where(row == 0, ends[0], ends[1]), 4 * velocities[i][2], 1))
    beside = collide(f, side[19] * (1.0 / LEVELS))
    ends = [jnp.broadcast_to(lines[k][19][0:1, :], (8, 128)) for k in range(2)]
    corner = collide(corner, jnp.where(row == 0, ends[0], ends[1]) * (1.0 / LEVELS))
    for k, (members, out) in enumerate(((forward, ahead), (backward, behind))):
        post = collide(lines[k][:19], lines[k][19] * (1.0 / LEVELS))
        for j, i in enumerate(members):
            step = velocities[i][1]
            value = roll(post[i], step, 1)
            if step:
                at, start = (0, 1) if step == 1 else (127, 2)
                spot = jnp.broadcast_to(corner[i][7 * k : 7 * k + 1, :], (8, 128))
                spot = jnp.where(lane == 4 * row + start, spot, 0.0)
                value = jnp.where(lane == at, jnp.sum(spot, axis=1, keepdims=True), value)
            out[j] = value

    for z in range(1, 7):
        f = []
        for i in range(19):
            value = arrived[i, z - 1]
            for members, k, at in ((forward, 0, 0), (backward, 1, 7)):
                if i in members:
                    entered = got[k][members.index(i)][z : z + 1, :]
                    value = jnp.where(row == at, jnp.broadcast_to(entered, (8, 128)), value)
            f.append(value)
        post = collide(f, codes[z].astype(F32) * (1.0 / LEVELS))
        for i in range(19):
            step = velocities[i][1]
            p2[i, z - 1] = mended(roll(post[i], step, 1), beside[i], step, z)


def last_kernel(p2, ahead, behind, planes, out, held_out, sems):
    lane, row = lanes(), rows()
    target = []
    for group in range(2):
        z, inner = (7, 6) if group == 0 else (0, 1)
        inward = sinking if group == 0 else rising
        target.append([(i, z) for i in level] + [(i, inner) for i in inward] + [(i, z) for i in inward])
    part = lane // 16
    for tile in range(5):
        held = [planes[h, tile] for h in range(8)]
        for k in (1, 2, 4):
            fixed = part & k == 0
            for h in range(8):
                if h & k == 0:
                    lo, hi = held[h], held[h | k]
                    held[h] = jnp.where(fixed, lo, roll(hi, 16 * k, 1))
                    held[h | k] = jnp.where(fixed, roll(lo, -16 * k, 1), hi)
        for slot in range(8):
            n = tile * 4 + 2 * (slot // 4) + slot % 2
            if n < 19:
                i, z = target[0 if slot % 4 >= 2 else 1][n]
                held_out[i, z] = held[slot] * weight_inverse[i]
    copies = []
    for i in range(19):
        for z in range(8):
            source = z - velocities[i][2]
            if 1 <= source <= 6:
                value = moved_x(p2[i, source - 1], i, source, lambda j: ahead[j], lambda j: behind[j], row)
                held_out[i, z] = value * weight_inverse[i]
        if i % 5 == 4 or i == 18:
            start = i - i % 5
            part = pl.ds(start, i + 1 - start)
            copies.append(pltpu.make_async_copy(held_out.at[part], out.at[part], sems.at[i // 5]))
            copies[-1].start()
    for copy in copies:
        copy.wait()


def run(kernel, outs, args, scratch=(), words=(), far_in=0, far_out=False, sems=0):
    near = pl.BlockSpec(memory_space=pltpu.VMEM)
    away = pl.BlockSpec(memory_space=pltpu.HBM)
    return pl.pallas_call(
        kernel,
        out_shape=[s if isinstance(s, jax.ShapeDtypeStruct) else jax.ShapeDtypeStruct(s, F32) for s in outs],
        in_specs=[away] * far_in + [near] * (len(args) - far_in),
        out_specs=[away if far_out else near] * len(outs),
        scratch_shapes=[pltpu.VMEM(s, F32) for s in scratch]
        + [pltpu.SMEM(s, jnp.int32) for s in words]
        + [pltpu.SemaphoreType.DMA((sems,))] * (sems > 0),
        compiler_params=pltpu.CompilerParams(vmem_limit_bytes=32 * 1024 * 1024),
    )(*args)


def neighbours(value_up, value_down, axis):
    peers = lax.axis_size(axis)
    up = [(i, (i + 1) % peers) for i in range(peers)]
    down = [(j, i) for i, j in up]
    return lax.ppermute(value_up, axis, up), lax.ppermute(value_down, axis, down)


def swaps(to_near, to_far, axis):
    peers = lax.axis_size(axis)
    pair = [(i, i ^ 1) for i in range(peers)]
    other = [(i, (i + peers - 1) % peers if i % 2 == 0 else (i + 1) % peers) for i in range(peers)]
    far = lax.ppermute(to_far, axis, other)
    near = lax.ppermute(to_near, axis, pair)
    return near, far


def body(pops, codes, offsets, fractions):
    tile = (8, 128)
    pops, codes, offsets, fractions = (
        pltpu.with_memory_space_constraint(value, pltpu.HBM) for value in (pops, codes, offsets, fractions)
    )
    edges, pops, codes = run(
        edge_kernel,
        [(5,) + tile, (19, 8) + tile, jax.ShapeDtypeStruct((8,) + tile, jnp.int32)],
        (pops, codes),
        far_in=2,
        sems=2,
    )
    near, far = swaps(edges, edges, "gy")
    p1, wrapped, middle, sides, params = run(
        main_kernel,
        [(19, 8) + tile, (10,) + tile, (6, 6) + tile, (2, 20) + tile, tile],
        (offsets, fractions, pops, codes),
        far_in=2,
        words=[offsets.shape] * 2,
        sems=2,
    )
    chunks, post_side, side, sent_ahead, sent_behind = run(
        edge_kernel_2,
        [(8, 6) + tile, (20,) + tile, (20,) + tile, (20,) + tile, (20,) + tile],
        (far, near, p1, codes, wrapped, middle, sides),
    )
    from_behind, from_ahead = neighbours(sent_ahead, sent_behind, "gx")
    own = lax.all_to_all(chunks, "gx", 0, 0)
    near, far = swaps(own[:, 0:3], own[:, 3:6], "gz")
    (spread,) = run(spread_kernel, [(20, 64, 128)], (own,))
    (arrived,) = run(arrive_kernel, [(19, 6) + tile], (p1, post_side))
    p2, ahead, behind = run(
        inner_kernel,
        [(19, 6) + tile, (5,) + tile, (5,) + tile],
        (arrived, side, codes, sent_ahead, sent_behind, from_behind, from_ahead),
    )
    (planes,) = run(
        plane_kernel,
        [(8, 5) + tile],
        (params, spread, far, near),
        scratch=[(20, 64, 128), (19, 64, 128)],
    )
    planes = lax.all_to_all(planes, "gx", 0, 0)
    (out,) = run(
        last_kernel, [(19, 8) + tile], (p2, ahead, behind, planes), scratch=[(19, 8) + tile], far_out=True, sems=4
    )
    return out


def solution(mesh):
    in_specs = (P(None, "gz", "gx", "gy"), P("gz", "gx", "gy"), P(), P())
    out_specs = P(None, "gz", "gx", "gy")
    return jax.shard_map(body, mesh=mesh, in_specs=in_specs, out_specs=out_specs, check_vma=False)
```
